256 devices in a mesh: seq: 16 (over y, x_lo, core), head: 16 (over x_hi, z).
Axes of the slice: x: 4 (x_hi: 2, x_lo: 2; x = x_hi * 2 + x_lo), y: 4, z: 8, core: 2. Of those that a mesh axis runs over, the one named last changes fastest.
Arguments:
- queries: bfloat16 [16384, 4096], P('seq', 'head'), may hold values from -8 to 8
- key_states: bfloat16 [2048, 4096], P('seq', 'head'), may hold values from -8 to 8
- value_states: bfloat16 [2048, 4096], P('seq', 'head'), may hold values from -6 to 6
- grad_out: bfloat16 [16384, 4096], P('seq', 'head'), may hold values from -6 to 6
- key_weight: bfloat16 [4096, 4096], P(None, 'head'), may hold values from -0.09375 to 0.09375
- value_weight: bfloat16 [4096, 4096], P(None, 'head'), may hold values from -0.09375 to 0.09375
- wait_lag: int32 [1], replicated, may hold values from 1 to 255
- target_offset: int32 [16], replicated, may hold values from 0 to 15360, as said below
- source_offset: int32 [16], replicated, may hold values from 0 to 1920, as said below
Outputs:
- query_grad: bfloat16 [16384, 4096], P('seq', 'head')
- memory_grad: bfloat16 [2048, 4096], P('seq', 'head')
The draws below stay inside these ranges and needn't reach their ends.
Inputs may be any that keep to these rules, and one draw needn't show every extreme that they name: `target_offset`: each entry is 1024 times a block number, every block number once. `source_offset`: each entry is 128 times a block number, every block number once.
All inputs are finite; a program needn't handle non-finite values.
Results may differ from the reference program's by a relative error of at most 0.0058.
Values may be sent and summed in bfloat16 or wider, within the bound.
A program may use at most 128 MiB of HBM per device.

```python
import jax
import jax.numpy as jnp
from jax import lax

D = 4096
HEADS = 64
HEAD_DIM = 64
TGT_DEV = 1024
SRC_DEV = 128
RATIO = 8
TGT = 16384
SRC = 2048
N_SEQ = 16


def source_order(key):
    return jax.random.permutation(jax.random.fold_in(key, 91), N_SEQ)


def draw_queries(key, part):
    key = jax.random.fold_in(key, 1)
    values = jnp.clip(jax.random.normal(key, (TGT, D), jnp.float32), -6.0, 6.0)
    return values.astype(jnp.bfloat16)


def draw_key_states(key, part):
    key = jax.random.fold_in(key, 2)
    values = jnp.clip(jax.random.normal(key, (SRC, D), jnp.float32), -6.0, 6.0)
    return values.astype(jnp.bfloat16)


def draw_target_offset(key, part):
    key = jax.random.fold_in(key, 5)
    return (jax.random.permutation(key, N_SEQ) * TGT_DEV).astype(jnp.int32)


def draw_source_offset(key, part):
    order = source_order(key)
    return (order * SRC_DEV).astype(jnp.int32)


def shard_levels(key, shape, pieces, low, top_value):
    factor_of = 1.0
    for dim, blocks in pieces:
        heights = jax.random.uniform(jax.random.fold_in(jax.random.fold_in(key, 6), dim), (blocks,), jnp.float32, low / len(pieces), top_value / len(pieces))
        factor_of = factor_of * jnp.repeat(jnp.exp(heights), shape[dim] // blocks).reshape((-1,) + (1,) * (len(shape) - 1 - dim))
    return factor_of


def gaussian(key, dims, spread, bound, pieces=(), kind=jnp.bfloat16):
    values = spread * jax.random.normal(key, dims, jnp.float32)
    if pieces:
        values = values * shard_levels(key, dims, pieces, -0.22, 0.18)
    return jnp.clip(values, -bound, bound).astype(kind)


def setup_inputs(seed: int = 0) -> dict:
    key_of = jax.random.split(jax.random.key(seed), 10)
    queries = draw_queries(jax.random.fold_in(key_of[9], 71), 0)
    key_states = draw_key_states(jax.random.fold_in(key_of[9], 71), 0)
    value_states = gaussian(key_of[2], (SRC, D), 1.0, 6.0, ((0, 16), (1, 16)))
    grad_out = gaussian(key_of[3], (TGT, D), 1.0, 6.0, ((0, 16), (1, 16)))
    key_weight = gaussian(key_of[4], (D, D), D ** -0.5, 0.09375, ((1, 16),))
    value_weight = gaussian(key_of[5], (D, D), D ** -0.5, 0.09375, ((1, 16),))
    wait_lag = jax.random.randint(key_of[6], (1,), 1, 2 * SRC_DEV).astype(jnp.int32)
    target_offset = draw_target_offset(jax.random.fold_in(key_of[9], 71), 0)
    source_offset = draw_source_offset(jax.random.fold_in(key_of[9], 71), 0)
    return {"queries": queries, "key_states": key_states, "value_states": value_states, "grad_out": grad_out, "key_weight": key_weight, "value_weight": value_weight, "wait_lag": wait_lag, "target_offset": target_offset, "source_offset": source_offset}


very_negative = -1e30


def heads_first(array):
    return array.reshape(array.shape[0], HEADS, HEAD_DIM).transpose(1, 0, 2)


def reference(queries, key_states, value_states, grad_out, key_weight, value_weight, wait_lag, target_offset, source_offset):
    score_scale = HEAD_DIM ** -0.5
    target_pos = jnp.repeat(target_offset, TGT_DEV) + jnp.tile(jnp.arange(TGT_DEV, dtype=jnp.int32), N_SEQ)
    source_pos = jnp.repeat(source_offset, SRC_DEV) + jnp.tile(jnp.arange(SRC_DEV, dtype=jnp.int32), N_SEQ)
    allowed = RATIO * source_pos[None, :] <= RATIO * wait_lag[0] + target_pos[:, None]

    def per_head(memory_total, inputs):
        query_head, key_head, value_head, grad_head, key_cols, value_cols = inputs
        logits = jnp.dot(query_head, key_head.T, preferred_element_type=jnp.float32) * score_scale
        row_max = jnp.max(jnp.where(allowed, logits, very_negative), axis=1)
        row_total = jnp.sum(jnp.where(allowed, jnp.exp(logits - row_max[:, None]), 0.0), axis=1)
        log_total = row_max + jnp.log(row_total)
        grad_probs = jnp.dot(grad_head, value_head.T, preferred_element_type=jnp.float32)
        probs = jnp.where(allowed, jnp.exp(logits - log_total[:, None]), 0.0)
        row_dots = jnp.sum(probs * grad_probs, axis=1)
        score_grad = probs * (grad_probs - row_dots[:, None])
        prob_half = probs.astype(jnp.bfloat16)
        grad_half = score_grad.astype(jnp.bfloat16)
        value_grad = jnp.dot(prob_half.T, grad_head, preferred_element_type=jnp.float32)
        key_grad = jnp.dot(grad_half.T, query_head, preferred_element_type=jnp.float32) * score_scale
        query_grad = (jnp.dot(grad_half, key_head, preferred_element_type=jnp.float32) * score_scale).astype(jnp.bfloat16)
        memory_total = memory_total + jnp.dot(key_grad.astype(jnp.bfloat16), key_cols.T, preferred_element_type=jnp.float32)
        memory_total = memory_total + jnp.dot(value_grad.astype(jnp.bfloat16), value_cols.T, preferred_element_type=jnp.float32)
        return memory_total, query_grad

    memory, head_grads = lax.scan(
        per_head,
        jnp.zeros((SRC, D), jnp.float32),
        (heads_first(queries), heads_first(key_states), heads_first(value_states), heads_first(grad_out),
         heads_first(key_weight), heads_first(value_weight)))
    query_grad = head_grads.transpose(1, 0, 2).reshape(TGT, D)
    return query_grad, memory.astype(jnp.bfloat16)
```

```python
import functools

import jax
import jax.numpy as jnp
from jax import lax
from jax.experimental import pallas as pl
from jax.experimental.pallas import tpu as pltpu
from jax.sharding import PartitionSpec as P

F32 = jnp.float32
BF16 = jnp.bfloat16
NEG = -1e30
HEADS, HD, TGT, SRC, SB, RATIO = 4, 64, 1024, 2048, 128, 8
FEAT = HEADS * HD
TILE = 512
CHUNK = 256
CHIPS = SRC // CHUNK
COLS = 256
NZ = 8
FAR_FIRST = (4, 3, 5, 2, 6, 1, 7, 0)
MESH = pl.DeviceIdType.MESH


def kernel(lag, toff, soff, q, g, k, v, wk_hbm, wv_hbm, dq, mem,
           qT, gT, qz, gz, kv, kT, s_ref, dp_ref, e_ref, acc, ds, dqT, part, sib, mid, rs, wk, wv, xs, xr, zs, zr,
           ag_s, ag_r, fw_s, fw_r, sb_s, sb_r, rs_s, rs_r, x_s, x_r, z_s, z_r, w_sem):
    me, head = lax.axis_index("seq"), lax.axis_index("head")
    y, xl, core = me // 4, lax.rem(me // 2, 2), lax.rem(me, 2)
    chip = me // 2
    xh, z = head // NZ, lax.rem(head, NZ)
    sibling = (chip * 2 + 1 - core, head)
    partner = (me, (1 - xh) * NZ + z)

    def chip_at(r, sign):
        return lax.rem(y + sign * (r // 2) + 4, 4) * 2 + (1 - xl if r % 2 else xl)

    def peer(r):
        return (chip_at(r, 1) * 2 + core, head)

    def z_at(r):
        return lax.rem(z + r, NZ)

    def z_peer(r):
        return (me, xh * NZ + z_at(r))

    barrier = pltpu.get_barrier_semaphore()
    for other in [sibling, partner] + [peer(r) for r in range(1, CHIPS)] + [z_peer(r) for r in range(1, NZ)]:
        pl.semaphore_signal(barrier, inc=1, device_id=other, device_id_type=MESH)

    def remote(src, dst, s_sem, r_sem, dev):
        return pltpu.make_async_remote_copy(src_ref=src, dst_ref=dst, send_sem=s_sem, recv_sem=r_sem, device_id=dev, device_id_type=MESH)

    def gather_out(h, r):
        return remote(kv.at[h, chip, core], kv.at[h, chip, core], ag_s.at[h, r], ag_r.at[h, r], peer(r))

    def gather_in(h, r):
        there = kv.at[h, chip_at(r, -1), core]
        return remote(there, there, ag_s.at[h, r], ag_r.at[h, r], peer(r))

    def forward(h):
        return remote(kv.at[h, :, core], kv.at[h, :, core], fw_s.at[h], fw_r.at[h], sibling)

    def forward_in(h):
        return remote(kv.at[h, :, 1 - core], kv.at[h, :, 1 - core], fw_s.at[h], fw_r.at[h], sibling)

    def to_sibling(h):
        return remote(part.at[h, :, 1 - core], sib.at[h], sb_s.at[h], sb_r.at[h], sibling)

    def scatter_out(h, r):
        return remote(mid.at[h, chip_at(r, 1)], rs.at[h, r], rs_s.at[h, r], rs_r.at[h, r], peer(r))

    def across(r):
        return remote(xs.at[r], xr.at[r], x_s.at[r], x_r.at[r], partner)

    def along(r):
        return remote(zs.at[r], zr.at[r], z_s.at[r], z_r.at[r], z_peer(r))

    load_k = pltpu.make_async_copy(wk_hbm, wk, w_sem.at[0])
    load_v = pltpu.make_async_copy(wv_hbm, wv, w_sem.at[1])
    load_k.start()
    load_v.start()

    low = lax.broadcasted_iota(jnp.int32, (1, 128), 1) < HD

    def swapped(a):
        return jnp.concatenate([a[:, HD:], a[:, :HD]], axis=1)

    for p in range(HEADS // 2):
        kp, vp = k[:, p * 128 : (p + 1) * 128], v[:, p * 128 : (p + 1) * 128]
        kv[2 * p, chip, core] = jnp.where(low, kp, swapped(vp))
        kv[2 * p + 1, chip, core] = jnp.where(low, swapped(kp), vp)

    pl.semaphore_wait(barrier, 16)
    for h in range(HEADS):
        for r in range(1, CHIPS):
            gather_out(h, r).start()

    for p in range(HEADS // 2):
        qp = q[:, p * 128 : (p + 1) * 128] * jnp.asarray(HD**-0.5, BF16)
        gp = g[:, p * 128 : (p + 1) * 128]
        qt, gt = qp.T, gp.T
        none = jnp.zeros_like(qp)
        zero = jnp.zeros((HD, TGT), BF16)
        qs, gs = swapped(qp), swapped(gp)
        for j in range(2):
            h = p * 2 + j
            qz[h] = jnp.where(low, qs if j else qp, none)
            gz[h] = jnp.where(low, none, gp if j else gs)
            qT[h, :HD, :] = qt[j * HD : (j + 1) * HD]
            qT[h, HD:, :] = zero
            gT[h, :HD, :] = zero
            gT[h, HD:, :] = gt[j * HD : (j + 1) * HD]

    def take_gathered(h):
        for r in range(1, CHIPS):
            gather_in(h, r).wait_recv()
        forward(h).start()

    def keys_ready(h):
        forward_in(h).wait_recv()
        kT[h] = kv[h].reshape(SRC, 128).T[:HD]

    def mid_step(h):
        to_sibling(h).wait_recv()
        mid[h] = (part[h, :, core].astype(F32) + sib[h].astype(F32)).astype(BF16)
        for r in range(1, CHIPS):
            scatter_out(h, r).start()

    take_gathered(0)
    keys_ready(0)

    def tile(h, i):
        ts = pl.ds(pl.multiple_of(i * TILE, TILE), TILE)
        reach = RATIO * lag[0] + toff[me] + i * TILE + lax.broadcasted_iota(jnp.int32, (1, TILE), 1)
        qt, gt = qT[h, :, ts], gT[h, :, ts]
        m = jnp.full((8, TILE), NEG, F32)
        for c in range(CHIPS):
            s = jnp.dot(kv[h, c].reshape(CHUNK, 128), qt, preferred_element_type=F32)
            for b in range(2):
                block = 2 * c + b
                pos = RATIO * soff[block] + RATIO * lax.broadcasted_iota(jnp.int32, (SB, TILE), 0)
                sb = jnp.where(pos <= reach, s[b * SB : (b + 1) * SB], NEG)
                s_ref[block * SB : (block + 1) * SB, :] = sb
                m = jnp.maximum(m, jnp.max(sb.reshape(SB // 8, 8, TILE), axis=0))
        m1 = jnp.max(m, axis=0, keepdims=True)
        l = jnp.zeros((8, TILE), F32)
        d = jnp.zeros((8, TILE), F32)
        for c in range(CHIPS):
            cs = slice(c * CHUNK, (c + 1) * CHUNK)
            dp = jnp.dot(kv[h, c].reshape(CHUNK, 128), gt, preferred_element_type=F32)
            e = jnp.exp(s_ref[cs, :] - m1)
            l = l + jnp.sum(e.reshape(CHUNK // 8, 8, TILE), axis=0)
            d = d + jnp.sum((e * dp).reshape(CHUNK // 8, 8, TILE), axis=0)
            e_ref[cs, :] = e
            dp_ref[cs, :] = dp
        inv = 1.0 / jnp.sum(l, axis=0, keepdims=True)
        dots = jnp.sum(d, axis=0, keepdims=True) * inv
        qzt, gzt = qz[h, ts, :], gz[h, ts, :]
        for c in range(CHIPS):
            cs = slice(c * CHUNK, (c + 1) * CHUNK)
            prob = e_ref[cs, :] * inv
            grad = (prob * (dp_ref[cs, :] - dots)).astype(BF16)
            ds[h, cs, ts] = grad
            acc[cs, :] += jnp.dot(prob.astype(BF16), gzt, preferred_element_type=F32) + jnp.dot(grad, qzt, preferred_element_type=F32)

    def query_grad(h):
        dqT[h] = jnp.dot(kT[h], ds[h], preferred_element_type=F32) * HD**-0.5

    @pl.loop(0, HEADS)
    def _(h):
        acc[...] = jnp.zeros_like(acc)

        @pl.loop(0, TGT // TILE)
        def _(i):
            @pl.when(i == 1)
            def _():
                @pl.when(h < HEADS - 1)
                def _():
                    take_gathered(h + 1)

                @pl.when(h > 0)
                def _():
                    mid_step(h - 1)

            tile(h, i)

        part[h] = acc[...].astype(BF16).reshape(CHIPS, 2, SB, 128)
        to_sibling(h).start()

        @pl.when(h < HEADS - 1)
        def _():
            keys_ready(h + 1)

    query_grad(0)
    mid_step(HEADS - 1)

    @pl.loop(1, HEADS)
    def _(h):
        query_grad(h)

    half = []
    for h in range(HEADS):
        total = mid[h, chip].astype(F32)
        for r in range(1, CHIPS):
            scatter_out(h, r).wait_recv()
            total = total + rs[h, r].astype(F32)
        half.append(total)

    half_k = jnp.concatenate([jnp.where(low, half[2 * p], swapped(half[2 * p + 1])) for p in range(2)], axis=1).astype(BF16)
    half_v = jnp.concatenate([jnp.where(low, swapped(half[2 * p]), half[2 * p + 1]) for p in range(2)], axis=1).astype(BF16)
    load_k.wait()
    load_v.wait()
    contract = (((1,), (1,)), ((), ()))

    def term(index):
        rows = pl.ds(pl.multiple_of(index * COLS, COLS), COLS)
        return lax.dot_general(half_k, wk[rows, :], contract, preferred_element_type=F32) + lax.dot_general(
            half_v, wv[rows, :], contract, preferred_element_type=F32
        )

    for r in FAR_FIRST:
        xs[r] = term((1 - xh) * NZ + z_at(r)).astype(BF16)
        across(r).start()
    for r in FAR_FIRST:
        own = term(xh * NZ + z_at(r))
        across(r).wait_recv()
        own = own + xr[r].astype(F32)
        if r:
            zs[r] = own.astype(BF16)
            along(r).start()
        else:
            total = own
    dq[...] = dqT[...].reshape(FEAT, TGT).T.astype(BF16)
    for r in (1, 7, 2, 6, 3, 5, 4):
        along(r).wait_recv()
        total = total + zr[r].astype(F32)
    mem[...] = total.astype(BF16)

    for h in range(HEADS):
        for r in range(1, CHIPS):
            gather_out(h, r).wait_send()
            scatter_out(h, r).wait_send()
        forward(h).wait_send()
        to_sibling(h).wait_send()
    for r in range(NZ):
        across(r).wait_send()
        if r:
            along(r).wait_send()


def attention(lag, toff, soff, q, g, k, v, wk, wv):
    vmem, smem, dma = pltpu.VMEM, pltpu.SMEM, pltpu.SemaphoreType.DMA
    return pl.pallas_call(
        kernel,
        out_shape=(jax.ShapeDtypeStruct((TGT, FEAT), BF16), jax.ShapeDtypeStruct((SB, COLS), BF16)),
        in_specs=[pl.BlockSpec(memory_space=smem)] * 3
        + [pl.BlockSpec(memory_space=vmem)] * 4
        + [pl.BlockSpec(memory_space=pl.ANY)] * 2,
        out_specs=(pl.BlockSpec(memory_space=vmem),) * 2,
        scratch_shapes=[
            vmem((HEADS, 128, TGT), BF16),
            vmem((HEADS, 128, TGT), BF16),
            vmem((HEADS, TGT, 128), BF16),
            vmem((HEADS, TGT, 128), BF16),
            vmem((HEADS, CHIPS, 2, SB, 128), BF16),
            vmem((HEADS, HD, SRC), BF16),
            vmem((SRC, TILE), F32),
            vmem((SRC, TILE), F32),
            vmem((SRC, TILE), F32),
            vmem((SRC, 128), F32),
            vmem((HEADS, SRC, TGT), BF16),
            vmem((HEADS, HD, TGT), F32),
            vmem((HEADS, CHIPS, 2, SB, 128), BF16),
            vmem((HEADS, CHIPS, SB, 128), BF16),
            vmem((HEADS, CHIPS, SB, 128), BF16),
            vmem((HEADS, CHIPS, SB, 128), BF16),
            vmem((16 * COLS, FEAT), BF16),
            vmem((16 * COLS, FEAT), BF16),
        ]
        + [vmem((NZ, SB, COLS), BF16)] * 4
        + [dma((HEADS, CHIPS))] * 2
        + [dma((HEADS,))] * 4
        + [dma((HEADS, CHIPS))] * 2
        + [dma((NZ,))] * 4
        + [dma((2,))],
        compiler_params=pltpu.CompilerParams(vmem_limit_bytes=58 * 2**20, collective_id=0, has_side_effects=True),
        name="wait_k_backward",
    )(lag, toff, soff, q, g, k, v, wk, wv)


def body(queries, key_states, value_states, grad_out, key_weight, value_weight, wait_lag, target_offset, source_offset):
    return attention(wait_lag, target_offset, source_offset, queries, grad_out, key_states, value_states, key_weight, value_weight)


def solution(mesh):
    rows = P("seq", "head")
    in_specs = (rows, rows, rows, rows, P(None, "head"), P(None, "head"), P(), P(), P())
    return jax.shard_map(body, mesh=mesh, in_specs=in_specs, out_specs=(rows, rows), check_vma=False)
```

```python
import functools

import jax
import jax.numpy as jnp
from jax import lax
from jax.experimental import pallas as pl
from jax.experimental.pallas import tpu as pltpu
from jax.sharding import PartitionSpec as P

F32 = jnp.float32
BF16 = jnp.bfloat16
NEG = -1e30
HEADS, HD, TGT, SRC, SB, RATIO = 4, 64, 1024, 2048, 128, 8
FEAT = HEADS * HD
TILE = 256
TILES = TGT // TILE
CHUNK = 256
CHIPS = SRC // CHUNK
COLS = 256
NZ = 8
FAR_FIRST = (4, 3, 5, 2, 6, 1, 7, 0)
NEAR = (1, 7, 2, 6)
MESH = pl.DeviceIdType.MESH


def kernel(lag, toff, soff, q, g, k, v, wk_hbm, wv_hbm, dq, mem,
           qT, gT, qz, gz, kv, kT, e_a, d_a, m_a, e_b, d_b, m_b, dots, acc, own, ds, dqT, part, sib, mid, rs, wk, wv, xs, xr, zs, zr, zl,
           ag_s, ag_r, fw_s, fw_r, sb_s, sb_r, rs_s, rs_r, x_s, x_r, z_s, z_r, l_r, w_sem):
    me, head = lax.axis_index("seq"), lax.axis_index("head")
    y, xl, core = me // 4, lax.rem(me // 2, 2), lax.rem(me, 2)
    chip = me // 2
    xh, z = head // NZ, lax.rem(head, NZ)
    sibling = (chip * 2 + 1 - core, head)
    partner = (me, (1 - xh) * NZ + z)

    def chip_at(r, sign):
        return lax.rem(y + sign * (r // 2) + 4, 4) * 2 + (1 - xl if r % 2 else xl)

    def peer(r):
        return (chip_at(r, 1) * 2 + core, head)

    def z_at(r):
        return lax.rem(z + r, NZ)

    def z_peer(r):
        return (me, xh * NZ + z_at(r))

    barrier = pltpu.get_barrier_semaphore()
    for other in [sibling, partner] + [peer(r) for r in range(1, CHIPS)] + [z_peer(r) for r in NEAR]:
        pl.semaphore_signal(barrier, inc=1, device_id=other, device_id_type=MESH)

    def remote(src, dst, s_sem, r_sem, dev):
        return pltpu.make_async_remote_copy(src_ref=src, dst_ref=dst, send_sem=s_sem, recv_sem=r_sem, device_id=dev, device_id_type=MESH)

    def gather_out(h, r):
        return remote(kv.at[h, chip, core], kv.at[h, chip, core], ag_s.at[h, r], ag_r.at[h, r], peer(r))

    def gather_in(h, r):
        there = kv.at[h, chip_at(r, -1), core]
        return remote(there, there, ag_s.at[h, r], ag_r.at[h, r], peer(r))

    def forward(h):
        return remote(kv.at[h, :, core], kv.at[h, :, core], fw_s.at[h], fw_r.at[h], sibling)

    def forward_in(h):
        return remote(kv.at[h, :, 1 - core], kv.at[h, :, 1 - core], fw_s.at[h], fw_r.at[h], sibling)

    def to_sibling(h):
        return remote(part.at[h, :, 1 - core], sib.at[h], sb_s.at[h], sb_r.at[h], sibling)

    def scatter_out(h, r):
        return remote(mid.at[h, chip_at(r, 1)], rs.at[h, r], rs_s.at[h, r], rs_r.at[h, r], peer(r))

    def across(r):
        return remote(xs.at[r], xr.at[r], x_s.at[r], x_r.at[r], partner)

    def along(r):
        return remote(zs.at[r], zr.at[r], z_s.at[r], z_r.at[r], z_peer(r))

    def relay(r):
        step = 2 + 4 * core if r == 4 else 1 if r == 3 else 7
        return remote(zs.at[r], zl.at[r - 3], z_s.at[r], l_r.at[r - 3], z_peer(step))

    load_k = pltpu.make_async_copy(wk_hbm, wk, w_sem.at[0])
    load_v = pltpu.make_async_copy(wv_hbm, wv, w_sem.at[1])
    load_k.start()
    load_v.start()

    low = lax.broadcasted_iota(jnp.int32, (1, 128), 1) < HD

    def swapped(a):
        return jnp.concatenate([a[:, HD:], a[:, :HD]], axis=1)

    for p in range(HEADS // 2):
        kp, vp = k[:, p * 128 : (p + 1) * 128], v[:, p * 128 : (p + 1) * 128]
        kv[2 * p, chip, core] = jnp.where(low, kp, swapped(vp))
        kv[2 * p + 1, chip, core] = jnp.where(low, swapped(kp), vp)

    def prepare(p):
        qp = q[:, p * 128 : (p + 1) * 128] * jnp.asarray(HD**-0.5, BF16)
        gp = g[:, p * 128 : (p + 1) * 128]
        qt, gt = qp.T, gp.T
        none = jnp.zeros_like(qp)
        zero = jnp.zeros((HD, TGT), BF16)
        qs, gs = swapped(qp), swapped(gp)
        for j in range(2):
            h = p * 2 + j
            qz[h] = jnp.where(low, qs if j else qp, none)
            gz[h] = jnp.where(low, none, gp if j else gs)
            qT[h, :HD, :] = qt[j * HD : (j + 1) * HD]
            qT[h, HD:, :] = zero
            gT[h, :HD, :] = zero
            gT[h, HD:, :] = gt[j * HD : (j + 1) * HD]

    prepare(0)
    pl.semaphore_wait(barrier, 13)
    for r in range(1, CHIPS):
        gather_out(0, r).start()
    prepare(1)

    def take_gathered(h):
        for r in range(1, CHIPS):
            gather_in(h, r).wait_recv()
        forward(h).start()

    def keys_ready(h):
        forward_in(h).wait_recv()

    def mid_step(h):
        to_sibling(h).wait_recv()
        mid[h] = (own[...] + sib[h].astype(F32)).astype(BF16)
        for r in range(1, CHIPS):
            scatter_out(h, r).start()

    take_gathered(0)

    @pl.loop(1, HEADS)
    def _(h):
        for r in range(1, CHIPS):
            gather_out(h, r).start()

    keys_ready(0)

    def first_half(h, i, e_ref, d_ref, m_ref):
        ts = pl.ds(pl.multiple_of(i * TILE, TILE), TILE)
        reach = RATIO * lag[0] + toff[me] + i * TILE + lax.broadcasted_iota(jnp.int32, (1, TILE), 1)
        step = RATIO * lax.broadcasted_iota(jnp.int32, (SB, TILE), 0)
        qt, gt = qT[h, :, ts], gT[h, :, ts]
        m = jnp.full((8, TILE), NEG, F32)
        l = jnp.zeros((8, TILE), F32)
        d = jnp.zeros((8, TILE), F32)
        for c in range(CHIPS):
            both = kv[h, c].reshape(CHUNK, 128)
            s = jnp.dot(both, qt, preferred_element_type=F32)
            dp = jnp.dot(both, gt, preferred_element_type=F32)
            for b in range(2):
                block = 2 * c + b
                rows = slice(block * SB, (block + 1) * SB)
                seen = jnp.where(step <= reach - RATIO * soff[block], s[b * SB : (b + 1) * SB], NEG).reshape(SB // 8, 8, TILE)
                grads = dp[b * SB : (b + 1) * SB].reshape(SB // 8, 8, TILE)
                new = jnp.maximum(m, jnp.max(seen, axis=0))
                scale = jnp.exp(m - new)
                e = jnp.exp(seen - new[None])
                l = l * scale + jnp.sum(e, axis=0)
                d = d * scale + jnp.sum(e * grads, axis=0)
                m = new
                e_ref[rows, :] = e.reshape(SB, TILE)
                d_ref[rows, :] = grads.reshape(SB, TILE)
                m_ref[block] = m
            yield
        top = jnp.max(m, axis=0, keepdims=True)
        weight = jnp.exp(m - top)
        inv = 1.0 / jnp.sum(l * weight, axis=0, keepdims=True)
        yield jnp.broadcast_to(jnp.sum(d * weight, axis=0, keepdims=True) * inv, (8, TILE))
        for block in range(2 * CHIPS):
            m_ref[block] = jnp.exp(m_ref[block] - top) * inv

    def second_half(h, i, e_ref, d_ref, m_ref, dot):
        ts = pl.ds(pl.multiple_of(i * TILE, TILE), TILE)
        qzt, gzt = qz[h, ts, :], gz[h, ts, :]
        for c in range(CHIPS):
            probs, grads = [], []
            for b in range(2):
                block = 2 * c + b
                rows = slice(block * SB, (block + 1) * SB)
                prob = e_ref[rows, :].reshape(SB // 8, 8, TILE) * m_ref[block][None]
                grad = prob * (d_ref[rows, :].reshape(SB // 8, 8, TILE) - dot[None])
                probs.append(prob.reshape(SB, TILE).astype(BF16))
                grads.append(grad.reshape(SB, TILE).astype(BF16))
            cs = slice(c * CHUNK, (c + 1) * CHUNK)
            prob, grad = jnp.concatenate(probs, axis=0), jnp.concatenate(grads, axis=0)
            ds[h, cs, ts] = grad
            acc[cs, :] += jnp.dot(prob, gzt, preferred_element_type=F32) + jnp.dot(grad, qzt, preferred_element_type=F32)
            yield

    slot_a, slot_b = (e_a, d_a, m_a), (e_b, d_b, m_b)

    def step(ahead, behind):
        one = first_half(ahead[0], ahead[1], *ahead[2]) if ahead else None
        two = second_half(behind[0], behind[1], *behind[2], dots[behind[3]]) if behind else None
        for c in range(CHIPS):
            if one:
                next(one)
            if two:
                next(two)
        if one:
            dots[ahead[3]] = next(one)
            next(one, None)

    step((0, 0, slot_a, 0), None)

    def query_grad(h):
        kT[...] = kv[h].reshape(SRC, 128).T[:HD]
        dqT[h] = jnp.dot(kT[...], ds[h], preferred_element_type=F32) * HD**-0.5

    @pl.loop(0, HEADS)
    def _(h):
        acc[...] = jnp.zeros_like(acc)

        @pl.loop(0, TILES // 2)
        def _(u):
            @pl.when(u == 1)
            def _():
                @pl.when(h < HEADS - 1)
                def _():
                    take_gathered(h + 1)

                @pl.when(h > 0)
                def _():
                    mid_step(h - 1)

            step((h, 2 * u + 1, slot_b, 1), (h, 2 * u, slot_a, 0))

            @pl.when(jnp.logical_and(u == 1, h < HEADS - 1))
            def _():
                keys_ready(h + 1)

            after = jnp.minimum(h * TILES + 2 * u + 2, HEADS * TILES - 1)
            step((after // TILES, lax.rem(after, TILES), slot_a, 0), (h, 2 * u + 1, slot_b, 1))

        both = acc[...].reshape(CHIPS, 2, SB, 128)
        part[h] = both.astype(BF16)
        own[...] = jnp.where(core == 0, both[:, 0], both[:, 1])
        to_sibling(h).start()

    query_grad(0)
    mid_step(HEADS - 1)

    @pl.loop(1, HEADS)
    def _(h):
        query_grad(h)

    half = []
    for h in range(HEADS):
        total = mid[h, chip].astype(F32)
        for r in range(1, CHIPS):
            scatter_out(h, r).wait_recv()
            total = total + rs[h, r].astype(F32)
        half.append(total)

    half_k = jnp.concatenate([jnp.where(low, half[2 * p], swapped(half[2 * p + 1])) for p in range(2)], axis=1).astype(BF16)
    half_v = jnp.concatenate([jnp.where(low, swapped(half[2 * p]), half[2 * p + 1]) for p in range(2)], axis=1).astype(BF16)
    load_k.wait()
    load_v.wait()
    contract = (((1,), (1,)), ((), ()))

    def term(index):
        rows = pl.ds(pl.multiple_of(index * COLS, COLS), COLS)
        return lax.dot_general(half_k, wk[rows, :], contract, preferred_element_type=F32) + lax.dot_general(
            half_v, wv[rows, :], contract, preferred_element_type=F32
        )

    for r in FAR_FIRST:
        xs[r] = term((1 - xh) * NZ + z_at(r)).astype(BF16)
        across(r).start()
    for r in FAR_FIRST:
        mine = term(xh * NZ + z_at(r))
        across(r).wait_recv()
        mine = mine + xr[r].astype(F32)
        if r in (3, 4, 5):
            zs[r] = mine.astype(BF16)
            relay(r).start()
            continue
        if r == 2:
            relay(3).wait_recv()
            relay(4).wait_recv()
            far = zl[1].astype(F32)
            mine = mine + zl[0].astype(F32) + jnp.where(core == 0, far, 0.0)
        if r == 6:
            relay(5).wait_recv()
            mine = mine + zl[2].astype(F32) + jnp.where(core == 1, far, 0.0)
        if r:
            zs[r] = mine.astype(BF16)
            along(r).start()
        else:
            total = mine
    dq[...] = dqT[...].reshape(FEAT, TGT).T.astype(BF16)
    for r in NEAR:
        along(r).wait_recv()
        total = total + zr[r].astype(F32)
    mem[...] = total.astype(BF16)

    for h in range(HEADS):
        for r in range(1, CHIPS):
            gather_out(h, r).wait_send()
            scatter_out(h, r).wait_send()
        forward(h).wait_send()
        to_sibling(h).wait_send()
    for r in range(NZ):
        across(r).wait_send()
        if r in NEAR:
            along(r).wait_send()
        elif r:
            relay(r).wait_send()


def attention(lag, toff, soff, q, g, k, v, wk, wv):
    vmem, smem, dma = pltpu.VMEM, pltpu.SMEM, pltpu.SemaphoreType.DMA
    return pl.pallas_call(
        kernel,
        out_shape=(jax.ShapeDtypeStruct((TGT, FEAT), BF16), jax.ShapeDtypeStruct((SB, COLS), BF16)),
        in_specs=[pl.BlockSpec(memory_space=smem)] * 3
        + [pl.BlockSpec(memory_space=vmem)] * 4
        + [pl.BlockSpec(memory_space=pl.ANY)] * 2,
        out_specs=(pl.BlockSpec(memory_space=vmem),) * 2,
        scratch_shapes=[
            vmem((HEADS, 128, TGT), BF16),
            vmem((HEADS, 128, TGT), BF16),
            vmem((HEADS, TGT, 128), BF16),
            vmem((HEADS, TGT, 128), BF16),
            vmem((HEADS, CHIPS, 2, SB, 128), BF16),
            vmem((HD, SRC), BF16),
        ]
        + [vmem((SRC, TILE), F32), vmem((SRC, TILE), F32), vmem((2 * CHIPS, 8, TILE), F32)] * 2
        + [
            vmem((2, 8, TILE), F32),
            vmem((SRC, 128), F32),
            vmem((CHIPS, SB, 128), F32),
            vmem((HEADS, SRC, TGT), BF16),
            vmem((HEADS, HD, TGT), F32),
            vmem((HEADS, CHIPS, 2, SB, 128), BF16),
            vmem((HEADS, CHIPS, SB, 128), BF16),
            vmem((HEADS, CHIPS, SB, 128), BF16),
            vmem((HEADS, CHIPS, SB, 128), BF16),
            vmem((16 * COLS, FEAT), BF16),
            vmem((16 * COLS, FEAT), BF16),
        ]
        + [vmem((NZ, SB, COLS), BF16)] * 4
        + [vmem((3, SB, COLS), BF16)]
        + [dma((HEADS, CHIPS))] * 2
        + [dma((HEADS,))] * 4
        + [dma((HEADS, CHIPS))] * 2
        + [dma((NZ,))] * 4
        + [dma((3,)), dma((2,))],
        compiler_params=pltpu.CompilerParams(vmem_limit_bytes=58 * 2**20, collective_id=0, has_side_effects=True),
        name="wait_k_backward",
    )(lag, toff, soff, q, g, k, v, wk, wv)


def hand_over_kernel(dq_in, mem_in, dq, mem):
    dq[...] = dq_in[...]
    mem[...] = mem_in[...]


def hand_over(dq, mem):
    vmem = pl.BlockSpec(memory_space=pltpu.VMEM)
    return pl.pallas_call(
        hand_over_kernel,
        out_shape=(jax.ShapeDtypeStruct(dq.shape, dq.dtype), jax.ShapeDtypeStruct(mem.shape, mem.dtype)),
        in_specs=[vmem, vmem],
        out_specs=(vmem, vmem),
        name="hand_over",
    )(dq, mem)


def body(queries, key_states, value_states, grad_out, key_weight, value_weight, wait_lag, target_offset, source_offset):
    return hand_over(
        *attention(wait_lag, target_offset, source_offset, queries, grad_out, key_states, value_states, key_weight, value_weight)
    )


def solution(mesh):
    rows = P("seq", "head")
    in_specs = (rows, rows, rows, rows, P(None, "head"), P(None, "head"), P(), P(), P())
    return jax.shard_map(body, mesh=mesh, in_specs=in_specs, out_specs=(rows, rows), check_vma=False)
```

```python
import functools

import jax
import jax.numpy as jnp
from jax import lax
from jax.experimental import pallas as pl
from jax.experimental.pallas import tpu as pltpu
from jax.sharding import PartitionSpec as P

F32 = jnp.float32
BF16 = jnp.bfloat16
NEG = -1e30
HEADS, HD, TGT, SRC, SB, RATIO = 4, 64, 1024, 2048, 128, 8
FEAT = HEADS * HD
TILE = 256
TILES = TGT // TILE
CHUNK = 256
CHIPS = SRC // CHUNK
COLS = 256
NZ = 8
NEAR = (1, 7, 2, 6)
OWNERS = (5, 4, 3, 7, 2, 6, 1, 0)
LAG = 5
MESH = pl.DeviceIdType.MESH


def kernel(lag, toff, soff, q_hbm, g_hbm, k_hbm, v_hbm, wk_hbm, wv_hbm, dq, mem,
           q, g, k, v, qT, gT, qz, gz, kv, kT, e_a, d_a, m_a, e_b, d_b, m_b, dots, acc, own, ds, dqT, part, sib, mid, rs, wk, wv, xs, xr, zs, zr, zl, ys, yr,
           ag_s, ag_r, fw_s, fw_r, sb_s, sb_r, rs_s, rs_r, x_s, x_r, z_s, z_r, l_r, w_sem, y_s, y_r, c_s, c_r):
    me, head = lax.axis_index("seq"), lax.axis_index("head")
    y, xl, core = me // 4, lax.rem(me // 2, 2), lax.rem(me, 2)
    chip = me // 2
    xh, z = head // NZ, lax.rem(head, NZ)
    sibling = (chip * 2 + 1 - core, head)
    partner = (me, (1 - xh) * NZ + z)

    def chip_at(r, sign):
        return lax.rem(y + sign * (r // 2) + 4, 4) * 2 + (1 - xl if r % 2 else xl)

    def peer(r):
        return (chip_at(r, 1) * 2 + core, head)

    def z_at(r):
        return lax.rem(z + r, NZ)

    def z_peer(r):
        return (me, xh * NZ + z_at(r))

    loads = [
        pltpu.make_async_copy(src, dst, w_sem.at[n])
        for n, (src, dst) in enumerate(((k_hbm, k), (v_hbm, v), (q_hbm, q), (g_hbm, g), (wk_hbm, wk), (wv_hbm, wv)))
    ]
    barrier = pltpu.get_barrier_semaphore()
    for other in [sibling, partner] + [peer(r) for r in range(1, CHIPS)] + [z_peer(r) for r in NEAR]:
        pl.semaphore_signal(barrier, inc=1, device_id=other, device_id_type=MESH)
    for load in loads:
        load.start()

    def remote(src, dst, s_sem, r_sem, dev):
        return pltpu.make_async_remote_copy(src_ref=src, dst_ref=dst, send_sem=s_sem, recv_sem=r_sem, device_id=dev, device_id_type=MESH)

    def gather_out(h, r):
        return remote(kv.at[h, chip, core], kv.at[h, chip, core], ag_s.at[h, r], ag_r.at[h, r], peer(r))

    def gather_in(h, r):
        there = kv.at[h, chip_at(r, -1), core]
        return remote(there, there, ag_s.at[h, r], ag_r.at[h, r], peer(r))

    def forward(h):
        return remote(kv.at[h, :, core], kv.at[h, :, core], fw_s.at[h], fw_r.at[h], sibling)

    def forward_in(h):
        return remote(kv.at[h, :, 1 - core], kv.at[h, :, 1 - core], fw_s.at[h], fw_r.at[h], sibling)

    def to_sibling(h):
        return remote(part.at[h, :, 1 - core], sib.at[h], sb_s.at[h], sb_r.at[h], sibling)

    def scatter_out(h, r):
        return remote(mid.at[h, chip_at(r, 1)], rs.at[h, r], rs_s.at[h, r], rs_r.at[h, r], peer(r))

    def across(r):
        return remote(xs.at[r], xr.at[r], x_s.at[r], x_r.at[r], partner)

    def along(r):
        return remote(zs.at[r], zr.at[r], z_s.at[r], z_r.at[r], z_peer(r))

    def along_too(r):
        return remote(ys.at[r // 7], yr.at[r // 7], y_s.at[r // 7], y_r.at[r // 7], z_peer(r))

    def relay(r):
        step = 2 + 4 * core if r == 4 else 1 if r == 3 else 7
        return remote(zs.at[r], zl.at[r - 3], z_s.at[r], l_r.at[r - 3], z_peer(step))

    low = lax.broadcasted_iota(jnp.int32, (1, 128), 1) < HD

    def swapped(a):
        return jnp.concatenate([a[:, HD:], a[:, :HD]], axis=1)

    loads[0].wait()
    loads[1].wait()
    for p in range(HEADS // 2):
        kp, vp = k[:, p * 128 : (p + 1) * 128], v[:, p * 128 : (p + 1) * 128]
        kv[2 * p, chip, core] = jnp.where(low, kp, swapped(vp))
        kv[2 * p + 1, chip, core] = jnp.where(low, swapped(kp), vp)

    def prepare(p):
        qp = q[:, p * 128 : (p + 1) * 128] * jnp.asarray(HD**-0.5, BF16)
        gp = g[:, p * 128 : (p + 1) * 128]
        qt, gt = qp.T, gp.T
        none = jnp.zeros_like(qp)
        zero = jnp.zeros((HD, TGT), BF16)
        qs, gs = swapped(qp), swapped(gp)
        for j in range(2):
            h = p * 2 + j
            qz[h] = jnp.where(low, qs if j else qp, none)
            gz[h] = jnp.where(low, none, gp if j else gs)
            qT[h, :HD, :] = qt[j * HD : (j + 1) * HD]
            qT[h, HD:, :] = zero
            gT[h, :HD, :] = zero
            gT[h, HD:, :] = gt[j * HD : (j + 1) * HD]

    loads[2].wait()
    loads[3].wait()
    prepare(0)
    pl.semaphore_wait(barrier, 13)
    for r in range(1, CHIPS):
        gather_out(0, r).start()
    prepare(1)

    def take_gathered(h):
        for r in range(1, CHIPS):
            gather_in(h, r).wait_recv()
        forward(h).start()

    def keys_ready(h):
        forward_in(h).wait_recv()

    def mid_step(h):
        to_sibling(h).wait_recv()
        mid[h] = (own[...] + sib[h].astype(F32)).astype(BF16)
        for r in range(1, CHIPS):
            scatter_out(h, r).start()

    take_gathered(0)

    @pl.loop(1, HEADS)
    def _(h):
        for r in range(1, CHIPS):
            gather_out(h, r).start()

    keys_ready(0)

    def first_half(h, i, e_ref, d_ref, m_ref):
        ts = pl.ds(pl.multiple_of(i * TILE, TILE), TILE)
        reach = RATIO * lag[0] + toff[me] + i * TILE + lax.broadcasted_iota(jnp.int32, (1, TILE), 1)
        step = RATIO * lax.broadcasted_iota(jnp.int32, (SB, TILE), 0)
        qt, gt = qT[h, :, ts], gT[h, :, ts]
        m = jnp.full((8, TILE), NEG, F32)
        l = jnp.zeros((8, TILE), F32)
        d = jnp.zeros((8, TILE), F32)
        for c in range(CHIPS):
            both = kv[h, c].reshape(CHUNK, 128)
            s = jnp.dot(both, qt, preferred_element_type=F32)
            dp = jnp.dot(both, gt, preferred_element_type=F32)
            for b in range(2):
                block = 2 * c + b
                rows = slice(block * SB, (block + 1) * SB)
                seen = jnp.where(step <= reach - RATIO * soff[block], s[b * SB : (b + 1) * SB], NEG).reshape(SB // 8, 8, TILE)
                grads = dp[b * SB : (b + 1) * SB].reshape(SB // 8, 8, TILE)
                new = jnp.maximum(m, jnp.max(seen, axis=0))
                scale = jnp.exp(m - new)
                e = jnp.exp(seen - new[None])
                l = l * scale + jnp.sum(e, axis=0)
                d = d * scale + jnp.sum(e * grads, axis=0)
                m = new
                e_ref[rows, :] = e.reshape(SB, TILE)
                d_ref[rows, :] = grads.reshape(SB, TILE)
                m_ref[block] = m
            yield
        top = jnp.max(m, axis=0, keepdims=True)
        weight = jnp.exp(m - top)
        inv = 1.0 / jnp.sum(l * weight, axis=0, keepdims=True)
        yield jnp.broadcast_to(jnp.sum(d * weight, axis=0, keepdims=True) * inv, (8, TILE))
        for block in range(2 * CHIPS):
            m_ref[block] = jnp.exp(m_ref[block] - top) * inv

    def second_half(h, i, e_ref, d_ref, m_ref, dot):
        ts = pl.ds(pl.multiple_of(i * TILE, TILE), TILE)
        qzt, gzt = qz[h, ts, :], gz[h, ts, :]
        for c in range(CHIPS):
            probs, grads = [], []
            for b in range(2):
                block = 2 * c + b
                rows = slice(block * SB, (block + 1) * SB)
                prob = e_ref[rows, :].reshape(SB // 8, 8, TILE) * m_ref[block][None]
                grad = prob * (d_ref[rows, :].reshape(SB // 8, 8, TILE) - dot[None])
                probs.append(prob.reshape(SB, TILE).astype(BF16))
                grads.append(grad.reshape(SB, TILE).astype(BF16))
            cs = slice(c * CHUNK, (c + 1) * CHUNK)
            prob, grad = jnp.concatenate(probs, axis=0), jnp.concatenate(grads, axis=0)
            ds[h, cs, ts] = grad
            acc[cs, :] += jnp.dot(prob, gzt, preferred_element_type=F32) + jnp.dot(grad, qzt, preferred_element_type=F32)
            yield

    def last_chunk(c, e_ref, d_ref, m_ref, dot):
        ts = slice(TGT - TILE, TGT)
        probs, grads = [], []
        for b in range(2):
            block = 2 * c + b
            rows = pl.ds(pl.multiple_of(block * SB, SB), SB)
            prob = e_ref[rows, :].reshape(SB // 8, 8, TILE) * m_ref[block][None]
            grad = prob * (d_ref[rows, :].reshape(SB // 8, 8, TILE) - dot[None])
            probs.append(prob.reshape(SB, TILE).astype(BF16))
            grads.append(grad.reshape(SB, TILE).astype(BF16))
        cs = pl.ds(pl.multiple_of(c * CHUNK, CHUNK), CHUNK)
        prob, grad = jnp.concatenate(probs, axis=0), jnp.concatenate(grads, axis=0)
        ds[HEADS - 1, cs, ts] = grad
        value = jnp.dot(prob, gz[HEADS - 1, ts, :], preferred_element_type=F32)
        value = value + jnp.dot(grad, qz[HEADS - 1, ts, :], preferred_element_type=F32)
        return (acc[cs, :] + value).reshape(2, SB, 128)

    def chunk_out(r):
        c = chip_at(r, 1)
        return remote(part.at[HEADS - 1, c, 1 - core], sib.at[HEADS - 1, c], c_s.at[r], c_r.at[r], sibling)

    def pass_on(r):
        c = chip_at(r, 1)
        chunk_out(r).wait_recv()
        mid[HEADS - 1, c] = (own[c] + sib[HEADS - 1, c].astype(F32)).astype(BF16)
        if r:
            scatter_out(HEADS - 1, r).start()

    slot_a, slot_b = (e_a, d_a, m_a), (e_b, d_b, m_b)

    def step(ahead, behind):
        one = first_half(ahead[0], ahead[1], *ahead[2]) if ahead else None
        two = second_half(behind[0], behind[1], *behind[2], dots[behind[3]]) if behind else None
        for c in range(CHIPS):
            if one:
                next(one)
            if two:
                next(two)
        if one:
            dots[ahead[3]] = next(one)
            next(one, None)

    step((0, 0, slot_a, 0), None)

    def query_grad(h):
        kT[...] = kv[h].reshape(SRC, 128).T[:HD]
        dqT[h] = jnp.dot(kT[...], ds[h], preferred_element_type=F32) * HD**-0.5

    @pl.loop(0, HEADS)
    def _(h):
        acc[...] = jnp.zeros_like(acc)

        @pl.loop(0, TILES // 2)
        def _(u):
            @pl.when(u == 1)
            def _():
                @pl.when(h < HEADS - 1)
                def _():
                    take_gathered(h + 1)

                @pl.when(h > 0)
                def _():
                    mid_step(h - 1)

            step((h, 2 * u + 1, slot_b, 1), (h, 2 * u, slot_a, 0))

            @pl.when(jnp.logical_and(u == 1, h < HEADS - 1))
            def _():
                keys_ready(h + 1)

            after = h * TILES + 2 * u + 2

            @pl.when(after < HEADS * TILES)
            def _():
                step((after // TILES, lax.rem(after, TILES), slot_a, 0), (h, 2 * u + 1, slot_b, 1))

        @pl.when(h < HEADS - 1)
        def _():
            both = acc[...].reshape(CHIPS, 2, SB, 128)
            part[h] = both.astype(BF16)
            own[...] = jnp.where(core == 0, both[:, 0], both[:, 1])
            to_sibling(h).start()

    last = HEADS - 1
    for n, r in enumerate(OWNERS):
        c = chip_at(r, 1)
        both = last_chunk(c, e_b, d_b, m_b, dots[1])
        part[last, c] = both.astype(BF16)
        own[c] = jnp.where(core == 0, both[0], both[1])
        chunk_out(r).start()
        if n >= LAG:
            pass_on(OWNERS[n - LAG])
    for r in OWNERS[CHIPS - LAG :]:
        pass_on(r)

    @pl.loop(0, HEADS)
    def _(h):
        query_grad(h)

    half = []
    for h in range(HEADS):
        total = mid[h, chip].astype(F32)
        for r in range(1, CHIPS):
            scatter_out(h, r).wait_recv()
            total = total + rs[h, r].astype(F32)
        half.append(total)

    half_k = jnp.concatenate([jnp.where(low, half[2 * p], swapped(half[2 * p + 1])) for p in range(2)], axis=1).astype(BF16)
    half_v = jnp.concatenate([jnp.where(low, swapped(half[2 * p]), half[2 * p + 1]) for p in range(2)], axis=1).astype(BF16)
    loads[4].wait()
    loads[5].wait()
    contract = (((1,), (1,)), ((), ()))

    def term(index):
        rows = pl.ds(pl.multiple_of(index * COLS, COLS), COLS)
        return lax.dot_general(half_k, wk[rows, :], contract, preferred_element_type=F32) + lax.dot_general(
            half_v, wv[rows, :], contract, preferred_element_type=F32
        )

    def send_across(r):
        xs[r] = term((1 - xh) * NZ + z_at(r)).astype(BF16)
        across(r).start()

    for r in (4, 3, 5):
        send_across(r)
    for r in (1, 7):
        zs[r] = term(xh * NZ + z_at(r)).astype(BF16)
        along(r).start()
        ys[r // 7] = term((1 - xh) * NZ + z_at(r)).astype(BF16)
        along_too(r).start()
    for r in (2, 6):
        send_across(r)
    for r in (4, 3, 5):
        mine = term(xh * NZ + z_at(r))
        across(r).wait_recv()
        zs[r] = (mine + xr[r].astype(F32)).astype(BF16)
        relay(r).start()
    mine = term((1 - xh) * NZ + z)
    for r in (1, 7):
        along_too(r).wait_recv()
        mine = mine + yr[r // 7].astype(F32)
    xs[0] = mine.astype(BF16)
    across(0).start()
    for r in (2, 6):
        mine = term(xh * NZ + z_at(r))
        across(r).wait_recv()
        mine = mine + xr[r].astype(F32)
        if r == 2:
            relay(3).wait_recv()
            relay(4).wait_recv()
            far = zl[1].astype(F32)
            mine = mine + zl[0].astype(F32) + jnp.where(core == 0, far, 0.0)
        else:
            relay(5).wait_recv()
            mine = mine + zl[2].astype(F32) + jnp.where(core == 1, far, 0.0)
        zs[r] = mine.astype(BF16)
        along(r).start()
    total = term(xh * NZ + z)
    dq[...] = dqT[...].reshape(FEAT, TGT).T.astype(BF16)
    across(0).wait_recv()
    total = total + xr[0].astype(F32)
    for r in NEAR:
        along(r).wait_recv()
        total = total + zr[r].astype(F32)
    mem[...] = total.astype(BF16)

    for h in range(HEADS):
        for r in range(1, CHIPS):
            gather_out(h, r).wait_send()
            scatter_out(h, r).wait_send()
        forward(h).wait_send()
    for h in range(HEADS - 1):
        to_sibling(h).wait_send()
    for r in range(CHIPS):
        chunk_out(r).wait_send()
    for r in (0, 2, 3, 4, 5, 6):
        across(r).wait_send()
    for r in NEAR:
        along(r).wait_send()
    for r in (3, 4, 5):
        relay(r).wait_send()
    for r in (1, 7):
        along_too(r).wait_send()


def attention(lag, toff, soff, q, g, k, v, wk, wv):
    vmem, smem, dma = pltpu.VMEM, pltpu.SMEM, pltpu.SemaphoreType.DMA
    return pl.pallas_call(
        kernel,
        out_shape=(jax.ShapeDtypeStruct((TGT, FEAT), BF16), jax.ShapeDtypeStruct((SB, COLS), BF16)),
        in_specs=[pl.BlockSpec(memory_space=smem)] * 3
        + [pl.BlockSpec(memory_space=pl.ANY)] * 6,
        out_specs=(pl.BlockSpec(memory_space=vmem),) * 2,
        scratch_shapes=[
            vmem((TGT, FEAT), BF16),
            vmem((TGT, FEAT), BF16),
            vmem((SB, FEAT), BF16),
            vmem((SB, FEAT), BF16),
            vmem((HEADS, 128, TGT), BF16),
            vmem((HEADS, 128, TGT), BF16),
            vmem((HEADS, TGT, 128), BF16),
            vmem((HEADS, TGT, 128), BF16),
            vmem((HEADS, CHIPS, 2, SB, 128), BF16),
            vmem((HD, SRC), BF16),
        ]
        + [vmem((SRC, TILE), F32), vmem((SRC, TILE), F32), vmem((2 * CHIPS, 8, TILE), F32)] * 2
        + [
            vmem((2, 8, TILE), F32),
            vmem((SRC, 128), F32),
            vmem((CHIPS, SB, 128), F32),
            vmem((HEADS, SRC, TGT), BF16),
            vmem((HEADS, HD, TGT), F32),
            vmem((HEADS, CHIPS, 2, SB, 128), BF16),
            vmem((HEADS, CHIPS, SB, 128), BF16),
            vmem((HEADS, CHIPS, SB, 128), BF16),
            vmem((HEADS, CHIPS, SB, 128), BF16),
            vmem((16 * COLS, FEAT), BF16),
            vmem((16 * COLS, FEAT), BF16),
        ]
        + [vmem((NZ, SB, COLS), BF16)] * 4
        + [vmem((3, SB, COLS), BF16)]
        + [vmem((2, SB, COLS), BF16)] * 2
        + [dma((HEADS, CHIPS))] * 2
        + [dma((HEADS,))] * 4
        + [dma((HEADS, CHIPS))] * 2
        + [dma((NZ,))] * 4
        + [dma((3,)), dma((6,))]
        + [dma((2,))] * 2
        + [dma((CHIPS,))] * 2,
        compiler_params=pltpu.CompilerParams(vmem_limit_bytes=58 * 2**20, collective_id=0, has_side_effects=True),
        name="wait_k_backward",
    )(lag, toff, soff, q, g, k, v, wk, wv)


def hand_over_kernel(dq_in, mem_in, dq, mem):
    dq[...] = dq_in[...]
    mem[...] = mem_in[...]


def hand_over(dq, mem):
    vmem = pl.BlockSpec(memory_space=pltpu.VMEM)
    return pl.pallas_call(
        hand_over_kernel,
        out_shape=(jax.ShapeDtypeStruct(dq.shape, dq.dtype), jax.ShapeDtypeStruct(mem.shape, mem.dtype)),
        in_specs=[vmem, vmem],
        out_specs=(vmem, vmem),
        name="hand_over",
    )(dq, mem)


def body(queries, key_states, value_states, grad_out, key_weight, value_weight, wait_lag, target_offset, source_offset):
    return hand_over(
        *attention(wait_lag, target_offset, source_offset, queries, grad_out, key_states, value_states, key_weight, value_weight)
    )


def solution(mesh):
    rows = P("seq", "head")
    in_specs = (rows, rows, rows, rows, P(None, "head"), P(None, "head"), P(), P(), P())
    return jax.shard_map(body, mesh=mesh, in_specs=in_specs, out_specs=(rows, rows), check_vma=False)
```

```python
import functools

import jax
import jax.numpy as jnp
from jax import lax
from jax.experimental import pallas as pl
from jax.experimental.pallas import tpu as pltpu
from jax.sharding import PartitionSpec as P

F32 = jnp.float32
BF16 = jnp.bfloat16
NEG = -1e30
HEADS, HD, TGT, SRC, SB, RATIO = 4, 64, 1024, 2048, 128, 8
FEAT = HEADS * HD
TILE = 256
TILES = TGT // TILE
CHUNK = 256
CHIPS = SRC // CHUNK
COLS = 256
NZ = 8
NEAR = (1, 7, 2, 6)
OWNERS = (5, 4, 3, 7, 2, 6, 1, 0)
LAG = 5
MESH = pl.DeviceIdType.MESH


def kernel(lag, toff, soff, q_hbm, g_hbm, k_hbm, v_hbm, wk_hbm, wv_hbm, dq, mem,
           q, g, k, v, qT, gT, qz, gz, kv, kT, e_a, d_a, m_a, e_b, d_b, m_b, dots, acc, own, ds, dqT, part, sib, mid, rs, wk, wv, xs, xr, zs, zr, zl, ys, yr,
           ag_s, ag_r, fw_s, fw_r, sb_s, sb_r, rs_s, rs_r, x_s, x_r, z_s, z_r, l_r, w_sem, y_s, y_r, c_s, c_r):
    me, head = lax.axis_index("seq"), lax.axis_index("head")
    y, xl, core = me // 4, lax.rem(me // 2, 2), lax.rem(me, 2)
    chip = me // 2
    xh, z = head // NZ, lax.rem(head, NZ)
    sibling = (chip * 2 + 1 - core, head)
    partner = (me, (1 - xh) * NZ + z)

    def chip_at(r, sign):
        return lax.rem(y + sign * (r // 2) + 4, 4) * 2 + (1 - xl if r % 2 else xl)

    def peer(r):
        return (chip_at(r, 1) * 2 + core, head)

    def z_at(r):
        return lax.rem(z + r, NZ)

    def z_peer(r):
        return (me, xh * NZ + z_at(r))

    loads = [
        pltpu.make_async_copy(src, dst, w_sem.at[n])
        for n, (src, dst) in enumerate(((k_hbm, k), (v_hbm, v), (q_hbm, q), (g_hbm, g), (wk_hbm, wk), (wv_hbm, wv)))
    ]
    barrier = pltpu.get_barrier_semaphore()
    for other in [sibling, partner] + [peer(r) for r in range(1, CHIPS)] + [z_peer(r) for r in NEAR]:
        pl.semaphore_signal(barrier, inc=1, device_id=other, device_id_type=MESH)
    for load in loads:
        load.start()

    def remote(src, dst, s_sem, r_sem, dev):
        return pltpu.make_async_remote_copy(src_ref=src, dst_ref=dst, send_sem=s_sem, recv_sem=r_sem, device_id=dev, device_id_type=MESH)

    def gather_out(h, r):
        return remote(kv.at[h, chip, core], kv.at[h, chip, core], ag_s.at[h, r], ag_r.at[h, r], peer(r))

    def gather_in(h, r):
        there = kv.at[h, chip_at(r, -1), core]
        return remote(there, there, ag_s.at[h, r], ag_r.at[h, r], peer(r))

    def forward(h):
        return remote(kv.at[h, :, core], kv.at[h, :, core], fw_s.at[h], fw_r.at[h], sibling)

    def forward_in(h):
        return remote(kv.at[h, :, 1 - core], kv.at[h, :, 1 - core], fw_s.at[h], fw_r.at[h], sibling)

    def to_sibling(h):
        return remote(part.at[h, :, 1 - core], sib.at[h], sb_s.at[h], sb_r.at[h], sibling)

    def scatter_out(h, r):
        return remote(mid.at[h, chip_at(r, 1)], rs.at[h, r], rs_s.at[h, r], rs_r.at[h, r], peer(r))

    def across(r):
        return remote(xs.at[r], xr.at[r], x_s.at[r], x_r.at[r], partner)

    def along(r):
        return remote(zs.at[r], zr.at[r], z_s.at[r], z_r.at[r], z_peer(r))

    def along_too(r):
        return remote(ys.at[r // 7], yr.at[r // 7], y_s.at[r // 7], y_r.at[r // 7], z_peer(r))

    def relay(r):
        step = 2 + 4 * core if r == 4 else 1 if r == 3 else 7
        return remote(zs.at[r], zl.at[r - 3], z_s.at[r], l_r.at[r - 3], z_peer(step))

    low = lax.broadcasted_iota(jnp.int32, (1, 128), 1) < HD

    def swapped(a):
        return jnp.concatenate([a[:, HD:], a[:, :HD]], axis=1)

    loads[0].wait()
    loads[1].wait()
    for p in range(HEADS // 2):
        kp, vp = k[:, p * 128 : (p + 1) * 128], v[:, p * 128 : (p + 1) * 128]
        kv[2 * p, chip, core] = jnp.where(low, kp, swapped(vp))
        kv[2 * p + 1, chip, core] = jnp.where(low, swapped(kp), vp)

    def prepare(p):
        qp = q[:, p * 128 : (p + 1) * 128] * jnp.asarray(HD**-0.5, BF16)
        gp = g[:, p * 128 : (p + 1) * 128]
        qt, gt = qp.T, gp.T
        none = jnp.zeros_like(qp)
        zero = jnp.zeros((HD, TGT), BF16)
        qs, gs = swapped(qp), swapped(gp)
        for j in range(2):
            h = p * 2 + j
            qz[h] = jnp.where(low, qs if j else qp, none)
            gz[h] = jnp.where(low, none, gp if j else gs)
            qT[h, :HD, :] = qt[j * HD : (j + 1) * HD]
            qT[h, HD:, :] = zero
            gT[h, :HD, :] = zero
            gT[h, HD:, :] = gt[j * HD : (j + 1) * HD]

    loads[2].wait()
    loads[3].wait()
    prepare(0)
    pl.semaphore_wait(barrier, 13)
    for r in range(1, CHIPS):
        gather_out(0, r).start()
    prepare(1)
    for r in range(1, CHIPS):
        gather_out(1, r).start()

    def take_gathered(h):
        for r in range(1, CHIPS):
            gather_in(h, r).wait_recv()
        forward(h).start()

    def keys_ready(h):
        forward_in(h).wait_recv()

    def mid_step(h):
        to_sibling(h).wait_recv()
        mid[h] = (own[...] + sib[h].astype(F32)).astype(BF16)
        for r in range(1, CHIPS):
            scatter_out(h, r).start()

    take_gathered(0)

    keys_ready(0)

    def first_half(h, i, e_ref, d_ref, m_ref):
        ts = pl.ds(pl.multiple_of(i * TILE, TILE), TILE)
        reach = RATIO * lag[0] + toff[me] + i * TILE + lax.broadcasted_iota(jnp.int32, (1, TILE), 1)
        step = RATIO * lax.broadcasted_iota(jnp.int32, (SB, TILE), 0)
        qt, gt = qT[h, :, ts], gT[h, :, ts]
        m = jnp.full((8, TILE), NEG, F32)
        l = jnp.zeros((8, TILE), F32)
        d = jnp.zeros((8, TILE), F32)
        for c in range(CHIPS):
            both = kv[h, c].reshape(CHUNK, 128)
            s = jnp.dot(both, qt, preferred_element_type=F32)
            dp = jnp.dot(both, gt, preferred_element_type=F32)
            for b in range(2):
                block = 2 * c + b
                rows = slice(block * SB, (block + 1) * SB)
                seen = jnp.where(step <= reach - RATIO * soff[block], s[b * SB : (b + 1) * SB], NEG).reshape(SB // 8, 8, TILE)
                grads = dp[b * SB : (b + 1) * SB].reshape(SB // 8, 8, TILE)
                new = jnp.maximum(m, jnp.max(seen, axis=0))
                scale = jnp.exp(m - new)
                e = jnp.exp(seen - new[None])
                l = l * scale + jnp.sum(e, axis=0)
                d = d * scale + jnp.sum(e * grads, axis=0)
                m = new
                e_ref[rows, :] = e.reshape(SB, TILE)
                d_ref[rows, :] = grads.reshape(SB, TILE)
                m_ref[block] = m
            yield
        top = jnp.max(m, axis=0, keepdims=True)
        weight = jnp.exp(m - top)
        inv = 1.0 / jnp.sum(l * weight, axis=0, keepdims=True)
        yield jnp.broadcast_to(jnp.sum(d * weight, axis=0, keepdims=True) * inv, (8, TILE))
        for block in range(2 * CHIPS):
            m_ref[block] = jnp.exp(m_ref[block] - top) * inv

    def second_half(h, i, e_ref, d_ref, m_ref, dot):
        ts = pl.ds(pl.multiple_of(i * TILE, TILE), TILE)
        qzt, gzt = qz[h, ts, :], gz[h, ts, :]
        for c in range(CHIPS):
            probs, grads = [], []
            for b in range(2):
                block = 2 * c + b
                rows = slice(block * SB, (block + 1) * SB)
                prob = e_ref[rows, :].reshape(SB // 8, 8, TILE) * m_ref[block][None]
                grad = prob * (d_ref[rows, :].reshape(SB // 8, 8, TILE) - dot[None])
                probs.append(prob.reshape(SB, TILE).astype(BF16))
                grads.append(grad.reshape(SB, TILE).astype(BF16))
            cs = slice(c * CHUNK, (c + 1) * CHUNK)
            prob, grad = jnp.concatenate(probs, axis=0), jnp.concatenate(grads, axis=0)
            ds[h, cs, ts] = grad
            acc[cs, :] += jnp.dot(prob, gzt, preferred_element_type=F32) + jnp.dot(grad, qzt, preferred_element_type=F32)
            yield

    def last_chunk(c, e_ref, d_ref, m_ref, dot):
        ts = slice(TGT - TILE, TGT)
        probs, grads = [], []
        for b in range(2):
            block = 2 * c + b
            rows = pl.ds(pl.multiple_of(block * SB, SB), SB)
            prob = e_ref[rows, :].reshape(SB // 8, 8, TILE) * m_ref[block][None]
            grad = prob * (d_ref[rows, :].reshape(SB // 8, 8, TILE) - dot[None])
            probs.append(prob.reshape(SB, TILE).astype(BF16))
            grads.append(grad.reshape(SB, TILE).astype(BF16))
        cs = pl.ds(pl.multiple_of(c * CHUNK, CHUNK), CHUNK)
        prob, grad = jnp.concatenate(probs, axis=0), jnp.concatenate(grads, axis=0)
        ds[HEADS - 1, cs, ts] = grad
        value = jnp.dot(prob, gz[HEADS - 1, ts, :], preferred_element_type=F32)
        value = value + jnp.dot(grad, qz[HEADS - 1, ts, :], preferred_element_type=F32)
        return (acc[cs, :] + value).reshape(2, SB, 128)

    def chunk_out(r):
        c = chip_at(r, 1)
        return remote(part.at[HEADS - 1, c, 1 - core], sib.at[HEADS - 1, c], c_s.at[r], c_r.at[r], sibling)

    def pass_on(r):
        c = chip_at(r, 1)
        chunk_out(r).wait_recv()
        mid[HEADS - 1, c] = (own[c] + sib[HEADS - 1, c].astype(F32)).astype(BF16)
        if r:
            scatter_out(HEADS - 1, r).start()

    slot_a, slot_b = (e_a, d_a, m_a), (e_b, d_b, m_b)

    def step(ahead, behind):
        one = first_half(ahead[0], ahead[1], *ahead[2]) if ahead else None
        two = second_half(behind[0], behind[1], *behind[2], dots[behind[3]]) if behind else None
        for c in range(CHIPS):
            if one:
                next(one)
            if two:
                next(two)
        if one:
            dots[ahead[3]] = next(one)
            next(one, None)

    step((0, 0, slot_a, 0), None)

    def query_grad(h):
        kT[...] = kv[h].reshape(SRC, 128).T[:HD]
        dqT[h] = jnp.dot(kT[...], ds[h], preferred_element_type=F32) * HD**-0.5

    @pl.loop(0, HEADS)
    def _(h):
        @pl.when(h < HEADS - 2)
        def _():
            for r in range(1, CHIPS):
                gather_out(h + 2, r).start()

        acc[...] = jnp.zeros_like(acc)

        @pl.loop(0, TILES // 2)
        def _(u):
            @pl.when(u == 1)
            def _():
                @pl.when(h < HEADS - 1)
                def _():
                    take_gathered(h + 1)

                @pl.when(h > 0)
                def _():
                    mid_step(h - 1)

            step((h, 2 * u + 1, slot_b, 1), (h, 2 * u, slot_a, 0))

            @pl.when(jnp.logical_and(u == 1, h < HEADS - 1))
            def _():
                keys_ready(h + 1)

            after = h * TILES + 2 * u + 2

            @pl.when(after < HEADS * TILES)
            def _():
                step((after // TILES, lax.rem(after, TILES), slot_a, 0), (h, 2 * u + 1, slot_b, 1))

        @pl.when(h < HEADS - 1)
        def _():
            both = acc[...].reshape(CHIPS, 2, SB, 128)
            part[h] = both.astype(BF16)
            own[...] = jnp.where(core == 0, both[:, 0], both[:, 1])
            to_sibling(h).start()

    last = HEADS - 1
    for n, r in enumerate(OWNERS):
        c = chip_at(r, 1)
        both = last_chunk(c, e_b, d_b, m_b, dots[1])
        part[last, c] = both.astype(BF16)
        own[c] = jnp.where(core == 0, both[0], both[1])
        chunk_out(r).start()
        if n >= LAG:
            pass_on(OWNERS[n - LAG])
    for r in OWNERS[CHIPS - LAG :]:
        pass_on(r)

    @pl.loop(0, HEADS)
    def _(h):
        query_grad(h)

    half = []
    for h in range(HEADS):
        total = mid[h, chip].astype(F32)
        for r in range(1, CHIPS):
            scatter_out(h, r).wait_recv()
            total = total + rs[h, r].astype(F32)
        half.append(total)

    half_k = jnp.concatenate([jnp.where(low, half[2 * p], swapped(half[2 * p + 1])) for p in range(2)], axis=1).astype(BF16)
    half_v = jnp.concatenate([jnp.where(low, swapped(half[2 * p]), half[2 * p + 1]) for p in range(2)], axis=1).astype(BF16)
    loads[4].wait()
    loads[5].wait()
    contract = (((1,), (1,)), ((), ()))

    def term(index):
        rows = pl.ds(pl.multiple_of(index * COLS, COLS), COLS)
        return lax.dot_general(half_k, wk[rows, :], contract, preferred_element_type=F32) + lax.dot_general(
            half_v, wv[rows, :], contract, preferred_element_type=F32
        )

    def send_across(r):
        xs[r] = term((1 - xh) * NZ + z_at(r)).astype(BF16)
        across(r).start()

    for r in (4, 3, 5):
        send_across(r)
    for r in (1, 7):
        zs[r] = term(xh * NZ + z_at(r)).astype(BF16)
        along(r).start()
        ys[r // 7] = term((1 - xh) * NZ + z_at(r)).astype(BF16)
        along_too(r).start()
    for r in (2, 6):
        send_across(r)
    for r in (4, 3, 5):
        mine = term(xh * NZ + z_at(r))
        across(r).wait_recv()
        zs[r] = (mine + xr[r].astype(F32)).astype(BF16)
        relay(r).start()
    mine = term((1 - xh) * NZ + z)
    for r in (1, 7):
        along_too(r).wait_recv()
        mine = mine + yr[r // 7].astype(F32)
    xs[0] = mine.astype(BF16)
    across(0).start()
    for r in (2, 6):
        mine = term(xh * NZ + z_at(r))
        across(r).wait_recv()
        mine = mine + xr[r].astype(F32)
        if r == 2:
            relay(3).wait_recv()
            relay(4).wait_recv()
            far = zl[1].astype(F32)
            mine = mine + zl[0].astype(F32) + jnp.where(core == 0, far, 0.0)
        else:
            relay(5).wait_recv()
            mine = mine + zl[2].astype(F32) + jnp.where(core == 1, far, 0.0)
        zs[r] = mine.astype(BF16)
        along(r).start()
    total = term(xh * NZ + z)
    dq[...] = dqT[...].reshape(FEAT, TGT).T.astype(BF16)
    across(0).wait_recv()
    total = total + xr[0].astype(F32)
    for r in NEAR:
        along(r).wait_recv()
        total = total + zr[r].astype(F32)
    mem[...] = total.astype(BF16)

    for h in range(HEADS):
        for r in range(1, CHIPS):
            gather_out(h, r).wait_send()
            scatter_out(h, r).wait_send()
        forward(h).wait_send()
    for h in range(HEADS - 1):
        to_sibling(h).wait_send()
    for r in range(CHIPS):
        chunk_out(r).wait_send()
    for r in (0, 2, 3, 4, 5, 6):
        across(r).wait_send()
    for r in NEAR:
        along(r).wait_send()
    for r in (3, 4, 5):
        relay(r).wait_send()
    for r in (1, 7):
        along_too(r).wait_send()


def attention(lag, toff, soff, q, g, k, v, wk, wv):
    vmem, smem, dma = pltpu.VMEM, pltpu.SMEM, pltpu.SemaphoreType.DMA
    return pl.pallas_call(
        kernel,
        out_shape=(jax.ShapeDtypeStruct((TGT, FEAT), BF16), jax.ShapeDtypeStruct((SB, COLS), BF16)),
        in_specs=[pl.BlockSpec(memory_space=smem)] * 3
        + [pl.BlockSpec(memory_space=pl.ANY)] * 6,
        out_specs=(pl.BlockSpec(memory_space=vmem),) * 2,
        scratch_shapes=[
            vmem((TGT, FEAT), BF16),
            vmem((TGT, FEAT), BF16),
            vmem((SB, FEAT), BF16),
            vmem((SB, FEAT), BF16),
            vmem((HEADS, 128, TGT), BF16),
            vmem((HEADS, 128, TGT), BF16),
            vmem((HEADS, TGT, 128), BF16),
            vmem((HEADS, TGT, 128), BF16),
            vmem((HEADS, CHIPS, 2, SB, 128), BF16),
            vmem((HD, SRC), BF16),
        ]
        + [vmem((SRC, TILE), F32), vmem((SRC, TILE), F32), vmem((2 * CHIPS, 8, TILE), F32)] * 2
        + [
            vmem((2, 8, TILE), F32),
            vmem((SRC, 128), F32),
            vmem((CHIPS, SB, 128), F32),
            vmem((HEADS, SRC, TGT), BF16),
            vmem((HEADS, HD, TGT), F32),
            vmem((HEADS, CHIPS, 2, SB, 128), BF16),
            vmem((HEADS, CHIPS, SB, 128), BF16),
            vmem((HEADS, CHIPS, SB, 128), BF16),
            vmem((HEADS, CHIPS, SB, 128), BF16),
            vmem((16 * COLS, FEAT), BF16),
            vmem((16 * COLS, FEAT), BF16),
        ]
        + [vmem((NZ, SB, COLS), BF16)] * 4
        + [vmem((3, SB, COLS), BF16)]
        + [vmem((2, SB, COLS), BF16)] * 2
        + [dma((HEADS, CHIPS))] * 2
        + [dma((HEADS,))] * 4
        + [dma((HEADS, CHIPS))] * 2
        + [dma((NZ,))] * 4
        + [dma((3,)), dma((6,))]
        + [dma((2,))] * 2
        + [dma((CHIPS,))] * 2,
        compiler_params=pltpu.CompilerParams(vmem_limit_bytes=58 * 2**20, collective_id=0, has_side_effects=True),
        name="wait_k_backward",
    )(lag, toff, soff, q, g, k, v, wk, wv)


def hand_over_kernel(dq_in, mem_in, dq, mem):
    dq[...] = dq_in[...]
    mem[...] = mem_in[...]


def hand_over(dq, mem):
    vmem = pl.BlockSpec(memory_space=pltpu.VMEM)
    return pl.pallas_call(
        hand_over_kernel,
        out_shape=(jax.ShapeDtypeStruct(dq.shape, dq.dtype), jax.ShapeDtypeStruct(mem.shape, mem.dtype)),
        in_specs=[vmem, vmem],
        out_specs=(vmem, vmem),
        name="hand_over",
    )(dq, mem)


def body(queries, key_states, value_states, grad_out, key_weight, value_weight, wait_lag, target_offset, source_offset):
    return hand_over(
        *attention(wait_lag, target_offset, source_offset, queries, grad_out, key_states, value_states, key_weight, value_weight)
    )


def solution(mesh):
    rows = P("seq", "head")
    in_specs = (rows, rows, rows, rows, P(None, "head"), P(None, "head"), P(), P(), P())
    return jax.shard_map(body, mesh=mesh, in_specs=in_specs, out_specs=(rows, rows), check_vma=False)
```

```python
import functools

import jax
import jax.numpy as jnp
from jax import lax
from jax.experimental import pallas as pl
from jax.experimental.pallas import tpu as pltpu
from jax.sharding import PartitionSpec as P

F32 = jnp.float32
BF16 = jnp.bfloat16
NEG = -1e30
HEADS, HD, TGT, SRC, SB, RATIO = 4, 64, 1024, 2048, 128, 8
FEAT = HEADS * HD
TILE = 256
TILES = TGT // TILE
CHUNK = 256
CHIPS = SRC // CHUNK
COLS = 256
NZ = 8
NEAR = (1, 7, 2, 6)
OWNERS = (5, 4, 3, 7, 2, 6, 1, 0)
LAG = 5
MESH = pl.DeviceIdType.MESH


def kernel(lag, toff, soff, q_hbm, g_hbm, k_hbm, v_hbm, wk_hbm, wv_hbm, dq, mem,
           q, g, k, v, qT, gT, qz, gz, kv, kT, e_a, d_a, m_a, e_b, d_b, m_b, dots, acc, own, ds, dqT, part, sib, mid, rs, wk, wv, xs, xr, zs, zr, zl, ys, yr,
           ag_s, ag_r, fw_s, fw_r, sb_s, sb_r, rs_s, rs_r, x_s, x_r, z_s, z_r, l_r, w_sem, y_s, y_r, c_s, c_r):
    me, head = lax.axis_index("seq"), lax.axis_index("head")
    y, xl, core = me // 4, lax.rem(me // 2, 2), lax.rem(me, 2)
    chip = me // 2
    xh, z = head // NZ, lax.rem(head, NZ)
    sibling = (chip * 2 + 1 - core, head)
    partner = (me, (1 - xh) * NZ + z)

    def chip_at(r, sign):
        return lax.rem(y + sign * (r // 2) + 4, 4) * 2 + (1 - xl if r % 2 else xl)

    def peer(r):
        return (chip_at(r, 1) * 2 + core, head)

    def z_at(r):
        return lax.rem(z + r, NZ)

    def z_peer(r):
        return (me, xh * NZ + z_at(r))

    loads = [
        pltpu.make_async_copy(src, dst, w_sem.at[n])
        for n, (src, dst) in enumerate(((k_hbm, k), (v_hbm, v), (q_hbm, q), (g_hbm, g), (wk_hbm, wk), (wv_hbm, wv)))
    ]
    barrier = pltpu.get_barrier_semaphore()
    for other in [sibling, partner] + [peer(r) for r in range(1, CHIPS)] + [z_peer(r) for r in NEAR]:
        pl.semaphore_signal(barrier, inc=1, device_id=other, device_id_type=MESH)
    for load in loads:
        load.start()

    def remote(src, dst, s_sem, r_sem, dev):
        return pltpu.make_async_remote_copy(src_ref=src, dst_ref=dst, send_sem=s_sem, recv_sem=r_sem, device_id=dev, device_id_type=MESH)

    def gather_out(h, r):
        return remote(kv.at[h, chip, core], kv.at[h, chip, core], ag_s.at[h, r], ag_r.at[h, r], peer(r))

    def gather_in(h, r):
        there = kv.at[h, chip_at(r, -1), core]
        return remote(there, there, ag_s.at[h, r], ag_r.at[h, r], peer(r))

    def forward(h):
        return remote(kv.at[h, :, core], kv.at[h, :, core], fw_s.at[h], fw_r.at[h], sibling)

    def forward_in(h):
        return remote(kv.at[h, :, 1 - core], kv.at[h, :, 1 - core], fw_s.at[h], fw_r.at[h], sibling)

    def to_sibling(h):
        return remote(part.at[h, :, 1 - core], sib.at[h], sb_s.at[h], sb_r.at[h], sibling)

    def scatter_out(h, r):
        return remote(mid.at[h, chip_at(r, 1)], rs.at[h, r], rs_s.at[h, r], rs_r.at[h, r], peer(r))

    def across(r):
        return remote(xs.at[r], xr.at[r], x_s.at[r], x_r.at[r], partner)

    def along(r):
        return remote(zs.at[r], zr.at[r], z_s.at[r], z_r.at[r], z_peer(r))

    def along_too(r):
        return remote(ys.at[r // 7], yr.at[r // 7], y_s.at[r // 7], y_r.at[r // 7], z_peer(r))

    def relay(r):
        step = 2 + 4 * core if r == 4 else 1 if r == 3 else 7
        return remote(zs.at[r], zl.at[r - 3], z_s.at[r], l_r.at[r - 3], z_peer(step))

    low = lax.broadcasted_iota(jnp.int32, (1, 128), 1) < HD

    def swapped(a):
        return jnp.concatenate([a[:, HD:], a[:, :HD]], axis=1)

    loads[0].wait()
    loads[1].wait()
    for p in range(HEADS // 2):
        kp, vp = k[:, p * 128 : (p + 1) * 128], v[:, p * 128 : (p + 1) * 128]
        kv[2 * p, chip, core] = jnp.where(low, kp, swapped(vp))
        kv[2 * p + 1, chip, core] = jnp.where(low, swapped(kp), vp)

    def prepare(p):
        qp = q[:, p * 128 : (p + 1) * 128] * jnp.asarray(HD**-0.5, BF16)
        gp = g[:, p * 128 : (p + 1) * 128]
        qt, gt = qp.T, gp.T
        none = jnp.zeros_like(qp)
        zero = jnp.zeros((HD, TGT), BF16)
        qs, gs = swapped(qp), swapped(gp)
        for j in range(2):
            h = p * 2 + j
            qz[h] = jnp.where(low, qs if j else qp, none)
            gz[h] = jnp.where(low, none, gp if j else gs)
            qT[h, :HD, :] = qt[j * HD : (j + 1) * HD]
            qT[h, HD:, :] = zero
            gT[h, :HD, :] = zero
            gT[h, HD:, :] = gt[j * HD : (j + 1) * HD]

    loads[2].wait()
    loads[3].wait()
    prepare(0)
    pl.semaphore_wait(barrier, 13)
    for r in range(1, CHIPS):
        gather_out(0, r).start()
    prepare(1)
    for r in range(1, CHIPS):
        gather_out(1, r).start()

    def take_gathered(h):
        for r in range(1, CHIPS):
            gather_in(h, r).wait_recv()
        forward(h).start()

    def keys_ready(h):
        forward_in(h).wait_recv()

    def mid_step(h):
        to_sibling(h).wait_recv()
        mid[h] = (own[...] + sib[h].astype(F32)).astype(BF16)
        for r in range(1, CHIPS):
            scatter_out(h, r).start()

    take_gathered(0)

    keys_ready(0)

    def first_half(h, i, e_ref, d_ref, m_ref):
        ts = pl.ds(pl.multiple_of(i * TILE, TILE), TILE)
        reach = RATIO * lag[0] + toff[me] + i * TILE + lax.broadcasted_iota(jnp.int32, (1, TILE), 1)
        step = RATIO * lax.broadcasted_iota(jnp.int32, (SB, TILE), 0)
        qt, gt = qT[h, :, ts], gT[h, :, ts]
        m = jnp.full((8, TILE), NEG, F32)
        l = jnp.zeros((8, TILE), F32)
        d = jnp.zeros((8, TILE), F32)
        for c in range(CHIPS):
            both = kv[h, c].reshape(CHUNK, 128)
            s = jnp.dot(both, qt, preferred_element_type=F32)
            dp = jnp.dot(both, gt, preferred_element_type=F32)
            for b in range(2):
                block = 2 * c + b
                rows = slice(block * SB, (block + 1) * SB)
                seen = jnp.where(step <= reach - RATIO * soff[block], s[b * SB : (b + 1) * SB], NEG).reshape(SB // 8, 8, TILE)
                grads = dp[b * SB : (b + 1) * SB].reshape(SB // 8, 8, TILE)
                new = jnp.maximum(m, jnp.max(seen, axis=0))
                scale = jnp.exp(m - new)
                e = jnp.exp(seen - new[None])
                l = l * scale + jnp.sum(e, axis=0)
                d = d * scale + jnp.sum(e * grads, axis=0)
                m = new
                e_ref[rows, :] = e.reshape(SB, TILE)
                d_ref[rows, :] = grads.reshape(SB, TILE)
                m_ref[block] = m
            yield
        top = jnp.max(m, axis=0, keepdims=True)
        weight = jnp.exp(m - top)
        inv = 1.0 / jnp.sum(l * weight, axis=0, keepdims=True)
        yield jnp.broadcast_to(jnp.sum(d * weight, axis=0, keepdims=True) * inv, (8, TILE))
        for block in range(2 * CHIPS):
            m_ref[block] = jnp.exp(m_ref[block] - top) * inv

    def second_half(h, i, e_ref, d_ref, m_ref, dot):
        ts = pl.ds(pl.multiple_of(i * TILE, TILE), TILE)
        qzt, gzt = qz[h, ts, :], gz[h, ts, :]
        for c in range(CHIPS):
            probs, grads = [], []
            for b in range(2):
                block = 2 * c + b
                rows = slice(block * SB, (block + 1) * SB)
                prob = e_ref[rows, :].reshape(SB // 8, 8, TILE) * m_ref[block][None]
                grad = prob * (d_ref[rows, :].reshape(SB // 8, 8, TILE) - dot[None])
                probs.append(prob.reshape(SB, TILE).astype(BF16))
                grads.append(grad.reshape(SB, TILE).astype(BF16))
            cs = slice(c * CHUNK, (c + 1) * CHUNK)
            prob, grad = jnp.concatenate(probs, axis=0), jnp.concatenate(grads, axis=0)
            ds[h, cs, ts] = grad
            acc[cs, :] += jnp.dot(prob, gzt, preferred_element_type=F32) + jnp.dot(grad, qzt, preferred_element_type=F32)
            yield

    def last_chunk(c, e_ref, d_ref, m_ref, dot):
        ts = slice(TGT - TILE, TGT)
        probs, grads = [], []
        for b in range(2):
            block = 2 * c + b
            rows = pl.ds(pl.multiple_of(block * SB, SB), SB)
            prob = e_ref[rows, :].reshape(SB // 8, 8, TILE) * m_ref[block][None]
            grad = prob * (d_ref[rows, :].reshape(SB // 8, 8, TILE) - dot[None])
            probs.append(prob.reshape(SB, TILE).astype(BF16))
            grads.append(grad.reshape(SB, TILE).astype(BF16))
        cs = pl.ds(pl.multiple_of(c * CHUNK, CHUNK), CHUNK)
        prob, grad = jnp.concatenate(probs, axis=0), jnp.concatenate(grads, axis=0)
        ds[HEADS - 1, cs, ts] = grad
        value = jnp.dot(prob, gz[HEADS - 1, ts, :], preferred_element_type=F32)
        value = value + jnp.dot(grad, qz[HEADS - 1, ts, :], preferred_element_type=F32)
        return (acc[cs, :] + value).reshape(2, SB, 128)

    def chunk_out(r):
        c = chip_at(r, 1)
        return remote(part.at[HEADS - 1, c, 1 - core], sib.at[HEADS - 1, c], c_s.at[r], c_r.at[r], sibling)

    def pass_on(r):
        c = chip_at(r, 1)
        chunk_out(r).wait_recv()
        mid[HEADS - 1, c] = (own[c] + sib[HEADS - 1, c].astype(F32)).astype(BF16)
        if r:
            scatter_out(HEADS - 1, r).start()

    slot_a, slot_b = (e_a, d_a, m_a), (e_b, d_b, m_b)

    def step(ahead, behind):
        one = first_half(ahead[0], ahead[1], *ahead[2]) if ahead else None
        two = second_half(behind[0], behind[1], *behind[2], dots[behind[3]]) if behind else None
        for c in range(CHIPS):
            if one:
                next(one)
            if two:
                next(two)
        if one:
            dots[ahead[3]] = next(one)
            next(one, None)

    step((0, 0, slot_a, 0), None)

    def query_grad(h):
        kT[...] = kv[h].reshape(SRC, 128).T[:HD]
        dqT[h] = jnp.dot(kT[...], ds[h], preferred_element_type=F32) * HD**-0.5

    @pl.loop(0, HEADS * TILES // 2 - 1)
    def _(n):
        h, u = n // 2, lax.rem(n, 2)

        @pl.when(u == 0)
        def _():
            @pl.when(h < HEADS - 2)
            def _():
                for r in range(1, CHIPS):
                    gather_out(h + 2, r).start()

            @pl.when(h < HEADS - 1)
            def _():
                take_gathered(h + 1)

            acc[...] = jnp.zeros_like(acc)

        @pl.when(u == 1)
        def _():
            keys_ready(h + 1)

            @pl.when(h > 0)
            def _():
                mid_step(h - 1)

        step((h, 2 * u + 1, slot_b, 1), (h, 2 * u, slot_a, 0))
        after = 2 * n + 2
        step((after // TILES, lax.rem(after, TILES), slot_a, 0), (h, 2 * u + 1, slot_b, 1))

        @pl.when(u == 1)
        def _():
            both = acc[...].reshape(CHIPS, 2, SB, 128)
            part[h] = both.astype(BF16)
            own[...] = jnp.where(core == 0, both[:, 0], both[:, 1])
            to_sibling(h).start()

    mid_step(HEADS - 2)
    step((HEADS - 1, TILES - 1, slot_b, 1), (HEADS - 1, TILES - 2, slot_a, 0))
    last = HEADS - 1
    for n, r in enumerate(OWNERS):
        c = chip_at(r, 1)
        both = last_chunk(c, e_b, d_b, m_b, dots[1])
        part[last, c] = both.astype(BF16)
        own[c] = jnp.where(core == 0, both[0], both[1])
        chunk_out(r).start()
        if n >= LAG:
            pass_on(OWNERS[n - LAG])
    for r in OWNERS[CHIPS - LAG :]:
        pass_on(r)

    @pl.loop(0, HEADS)
    def _(h):
        query_grad(h)

    half = []
    for h in range(HEADS):
        total = mid[h, chip].astype(F32)
        for r in range(1, CHIPS):
            scatter_out(h, r).wait_recv()
            total = total + rs[h, r].astype(F32)
        half.append(total.T)

    half_k = jnp.concatenate([t[:HD] for t in half], axis=0).astype(BF16)
    half_v = jnp.concatenate([t[HD:] for t in half], axis=0).astype(BF16)
    loads[4].wait()
    loads[5].wait()

    def term(index):
        rows = pl.ds(pl.multiple_of(index * COLS, COLS), COLS)
        return jnp.dot(wk[rows, :], half_k, preferred_element_type=F32) + jnp.dot(wv[rows, :], half_v, preferred_element_type=F32)

    def send_across(r):
        xs[r] = term((1 - xh) * NZ + z_at(r)).astype(BF16)
        across(r).start()

    for r in (4, 3, 5):
        send_across(r)
    for r in (1, 7):
        zs[r] = term(xh * NZ + z_at(r)).astype(BF16)
        along(r).start()
        ys[r // 7] = term((1 - xh) * NZ + z_at(r)).astype(BF16)
        along_too(r).start()
    for r in (2, 6):
        send_across(r)
    for r in (4, 3, 5):
        mine = term(xh * NZ + z_at(r))
        across(r).wait_recv()
        zs[r] = (mine + xr[r].astype(F32)).astype(BF16)
        relay(r).start()
    mine = term((1 - xh) * NZ + z)
    for r in (1, 7):
        along_too(r).wait_recv()
        mine = mine + yr[r // 7].astype(F32)
    xs[0] = mine.astype(BF16)
    across(0).start()
    for r in (2, 6):
        mine = term(xh * NZ + z_at(r))
        across(r).wait_recv()
        mine = mine + xr[r].astype(F32)
        if r == 2:
            relay(3).wait_recv()
            relay(4).wait_recv()
            far = zl[1].astype(F32)
            mine = mine + zl[0].astype(F32) + jnp.where(core == 0, far, 0.0)
        else:
            relay(5).wait_recv()
            mine = mine + zl[2].astype(F32) + jnp.where(core == 1, far, 0.0)
        zs[r] = mine.astype(BF16)
        along(r).start()
    total = term(xh * NZ + z)
    dq[...] = dqT[...].reshape(FEAT, TGT).T.astype(BF16)
    across(0).wait_recv()
    total = total + xr[0].astype(F32)
    for r in NEAR:
        along(r).wait_recv()
        total = total + zr[r].astype(F32)
    mem[...] = total.T.astype(BF16)

    for h in range(HEADS):
        for r in range(1, CHIPS):
            gather_out(h, r).wait_send()
            scatter_out(h, r).wait_send()
        forward(h).wait_send()
    for h in range(HEADS - 1):
        to_sibling(h).wait_send()
    for r in range(CHIPS):
        chunk_out(r).wait_send()
    for r in (0, 2, 3, 4, 5, 6):
        across(r).wait_send()
    for r in NEAR:
        along(r).wait_send()
    for r in (3, 4, 5):
        relay(r).wait_send()
    for r in (1, 7):
        along_too(r).wait_send()


def attention(lag, toff, soff, q, g, k, v, wk, wv):
    vmem, smem, dma = pltpu.VMEM, pltpu.SMEM, pltpu.SemaphoreType.DMA
    return pl.pallas_call(
        kernel,
        out_shape=(jax.ShapeDtypeStruct((TGT, FEAT), BF16), jax.ShapeDtypeStruct((SB, COLS), BF16)),
        in_specs=[pl.BlockSpec(memory_space=smem)] * 3
        + [pl.BlockSpec(memory_space=pl.ANY)] * 6,
        out_specs=(pl.BlockSpec(memory_space=vmem),) * 2,
        scratch_shapes=[
            vmem((TGT, FEAT), BF16),
            vmem((TGT, FEAT), BF16),
            vmem((SB, FEAT), BF16),
            vmem((SB, FEAT), BF16),
            vmem((HEADS, 128, TGT), BF16),
            vmem((HEADS, 128, TGT), BF16),
            vmem((HEADS, TGT, 128), BF16),
            vmem((HEADS, TGT, 128), BF16),
            vmem((HEADS, CHIPS, 2, SB, 128), BF16),
            vmem((HD, SRC), BF16),
        ]
        + [vmem((SRC, TILE), F32), vmem((SRC, TILE), F32), vmem((2 * CHIPS, 8, TILE), F32)] * 2
        + [
            vmem((2, 8, TILE), F32),
            vmem((SRC, 128), F32),
            vmem((CHIPS, SB, 128), F32),
            vmem((HEADS, SRC, TGT), BF16),
            vmem((HEADS, HD, TGT), F32),
            vmem((HEADS, CHIPS, 2, SB, 128), BF16),
            vmem((HEADS, CHIPS, SB, 128), BF16),
            vmem((HEADS, CHIPS, SB, 128), BF16),
            vmem((HEADS, CHIPS, SB, 128), BF16),
            vmem((16 * COLS, FEAT), BF16),
            vmem((16 * COLS, FEAT), BF16),
        ]
        + [vmem((NZ, COLS, SB), BF16)] * 4
        + [vmem((3, COLS, SB), BF16)]
        + [vmem((2, COLS, SB), BF16)] * 2
        + [dma((HEADS, CHIPS))] * 2
        + [dma((HEADS,))] * 4
        + [dma((HEADS, CHIPS))] * 2
        + [dma((NZ,))] * 4
        + [dma((3,)), dma((6,))]
        + [dma((2,))] * 2
        + [dma((CHIPS,))] * 2,
        compiler_params=pltpu.CompilerParams(vmem_limit_bytes=58 * 2**20, collective_id=0, has_side_effects=True),
        name="wait_k_backward",
    )(lag, toff, soff, q, g, k, v, wk, wv)


def hand_over_kernel(dq_in, mem_in, dq, mem):
    dq[...] = dq_in[...]
    mem[...] = mem_in[...]


def hand_over(dq, mem):
    vmem = pl.BlockSpec(memory_space=pltpu.VMEM)
    return pl.pallas_call(
        hand_over_kernel,
        out_shape=(jax.ShapeDtypeStruct(dq.shape, dq.dtype), jax.ShapeDtypeStruct(mem.shape, mem.dtype)),
        in_specs=[vmem, vmem],
        out_specs=(vmem, vmem),
        name="hand_over",
    )(dq, mem)


def body(queries, key_states, value_states, grad_out, key_weight, value_weight, wait_lag, target_offset, source_offset):
    return hand_over(
        *attention(wait_lag, target_offset, source_offset, queries, grad_out, key_states, value_states, key_weight, value_weight)
    )


def solution(mesh):
    rows = P("seq", "head")
    in_specs = (rows, rows, rows, rows, P(None, "head"), P(None, "head"), P(), P(), P())
    return jax.shard_map(body, mesh=mesh, in_specs=in_specs, out_specs=(rows, rows), check_vma=False)
```

```python
import functools

import jax
import jax.numpy as jnp
from jax import lax
from jax.experimental import pallas as pl
from jax.experimental.pallas import tpu as pltpu
from jax.sharding import PartitionSpec as P

F32 = jnp.float32
BF16 = jnp.bfloat16
NEG = -1e30
HEADS, HD, TGT, SRC, SB, RATIO = 4, 64, 1024, 2048, 128, 8
FEAT = HEADS * HD
TILE = 256
TILES = TGT // TILE
CHUNK = 256
CHIPS = SRC // CHUNK
COLS = 256
NZ = 8
NEAR = (1, 7, 2, 6)
OWNERS = (5, 4, 3, 7, 2, 6, 1, 0)
LAG = 5
MESH = pl.DeviceIdType.MESH


def kernel(lag, toff, soff, q_hbm, g_hbm, k_hbm, v_hbm, wk_hbm, wv_hbm, dq, mem,
           q, g, k, v, qT, gT, qz, gz, kv, kT, e_a, d_a, m_a, e_b, d_b, m_b, dots, acc, own, ds, dqT, part, sib, mid, rs, wk, wv, xs, xr, zs, zr, zl, ys, yr,
           ag_s, ag_r, fw_s, fw_r, sb_s, sb_r, rs_s, rs_r, x_s, x_r, z_s, z_r, l_r, w_sem, y_s, y_r, c_s, c_r):
    me, head = lax.axis_index("seq"), lax.axis_index("head")
    y, xl, core = me // 4, lax.rem(me // 2, 2), lax.rem(me, 2)
    chip = me // 2
    xh, z = head // NZ, lax.rem(head, NZ)
    sibling = (chip * 2 + 1 - core, head)
    partner = (me, (1 - xh) * NZ + z)

    def chip_at(r, sign):
        return lax.rem(y + sign * (r // 2) + 4, 4) * 2 + (1 - xl if r % 2 else xl)

    def peer(r):
        return (chip_at(r, 1) * 2 + core, head)

    def z_at(r):
        return lax.rem(z + r, NZ)

    def z_peer(r):
        return (me, xh * NZ + z_at(r))

    loads = [
        pltpu.make_async_copy(src, dst, w_sem.at[n])
        for n, (src, dst) in enumerate(((k_hbm, k), (v_hbm, v), (q_hbm, q), (g_hbm, g), (wk_hbm, wk), (wv_hbm, wv)))
    ]
    barrier = pltpu.get_barrier_semaphore()
    for other in [sibling, partner] + [peer(r) for r in range(1, CHIPS)] + [z_peer(r) for r in NEAR]:
        pl.semaphore_signal(barrier, inc=1, device_id=other, device_id_type=MESH)
    for load in loads:
        load.start()

    def remote(src, dst, s_sem, r_sem, dev):
        return pltpu.make_async_remote_copy(src_ref=src, dst_ref=dst, send_sem=s_sem, recv_sem=r_sem, device_id=dev, device_id_type=MESH)

    def gather_out(h, r):
        return remote(kv.at[h, chip, core], kv.at[h, chip, core], ag_s.at[h, r], ag_r.at[h, r], peer(r))

    def gather_in(h, r):
        there = kv.at[h, chip_at(r, -1), core]
        return remote(there, there, ag_s.at[h, r], ag_r.at[h, r], peer(r))

    def forward(h):
        return remote(kv.at[h, :, core], kv.at[h, :, core], fw_s.at[h], fw_r.at[h], sibling)

    def forward_in(h):
        return remote(kv.at[h, :, 1 - core], kv.at[h, :, 1 - core], fw_s.at[h], fw_r.at[h], sibling)

    def to_sibling(h):
        return remote(part.at[h, :, 1 - core], sib.at[h], sb_s.at[h], sb_r.at[h], sibling)

    def scatter_out(h, r):
        return remote(mid.at[h, chip_at(r, 1)], rs.at[h, r], rs_s.at[h, r], rs_r.at[h, r], peer(r))

    def across(r):
        return remote(xs.at[r], xr.at[r], x_s.at[r], x_r.at[r], partner)

    def along(r):
        return remote(zs.at[r], zr.at[r], z_s.at[r], z_r.at[r], z_peer(r))

    def along_too(r):
        return remote(ys.at[r // 7], yr.at[r // 7], y_s.at[r // 7], y_r.at[r // 7], z_peer(r))

    def relay(r):
        step = 2 + 4 * core if r == 4 else 1 if r == 3 else 7
        return remote(zs.at[r], zl.at[r - 3], z_s.at[r], l_r.at[r - 3], z_peer(step))

    low = lax.broadcasted_iota(jnp.int32, (1, 128), 1) < HD

    def swapped(a):
        return jnp.concatenate([a[:, HD:], a[:, :HD]], axis=1)

    loads[0].wait()
    loads[1].wait()
    for p in range(HEADS // 2):
        kp, vp = k[:, p * 128 : (p + 1) * 128], v[:, p * 128 : (p + 1) * 128]
        kv[2 * p, chip, core] = jnp.where(low, kp, swapped(vp))
        kv[2 * p + 1, chip, core] = jnp.where(low, swapped(kp), vp)

    def prepare(p):
        qp = q[:, p * 128 : (p + 1) * 128] * jnp.asarray(HD**-0.5, BF16)
        gp = g[:, p * 128 : (p + 1) * 128]
        qt, gt = qp.T, gp.T
        none = jnp.zeros_like(qp)
        zero = jnp.zeros((HD, TGT), BF16)
        qs, gs = swapped(qp), swapped(gp)
        for j in range(2):
            h = p * 2 + j
            qz[h] = jnp.where(low, qs if j else qp, none)
            gz[h] = jnp.where(low, none, gp if j else gs)
            qT[h, :HD, :] = qt[j * HD : (j + 1) * HD]
            qT[h, HD:, :] = zero
            gT[h, :HD, :] = zero
            gT[h, HD:, :] = gt[j * HD : (j + 1) * HD]

    loads[2].wait()
    loads[3].wait()
    prepare(0)
    pl.semaphore_wait(barrier, 13)
    for r in range(1, CHIPS):
        gather_out(0, r).start()
    prepare(1)
    for r in range(1, CHIPS):
        gather_out(1, r).start()

    def take_gathered(h):
        for r in range(1, CHIPS):
            gather_in(h, r).wait_recv()
        forward(h).start()

    def keys_ready(h):
        forward_in(h).wait_recv()

    def mid_step(h):
        to_sibling(h).wait_recv()
        mid[h] = (own[...] + sib[h].astype(F32)).astype(BF16)
        for r in range(1, CHIPS):
            scatter_out(h, r).start()

    take_gathered(0)

    keys_ready(0)

    def first_half(h, i, e_ref, d_ref, m_ref):
        ts = pl.ds(pl.multiple_of(i * TILE, TILE), TILE)
        reach = RATIO * lag[0] + toff[me] + i * TILE + lax.broadcasted_iota(jnp.int32, (1, TILE), 1)
        step = RATIO * lax.broadcasted_iota(jnp.int32, (SB, TILE), 0)
        qt, gt = qT[h, :, ts], gT[h, :, ts]
        m = jnp.full((8, TILE), NEG, F32)
        l = jnp.zeros((8, TILE), F32)
        d = jnp.zeros((8, TILE), F32)
        for c in range(CHIPS):
            both = kv[h, c].reshape(CHUNK, 128)
            s = jnp.dot(both, qt, preferred_element_type=F32)
            dp = jnp.dot(both, gt, preferred_element_type=F32)
            for b in range(2):
                block = 2 * c + b
                rows = slice(block * SB, (block + 1) * SB)
                seen = jnp.where(step <= reach - RATIO * soff[block], s[b * SB : (b + 1) * SB], NEG).reshape(SB // 8, 8, TILE)
                grads = dp[b * SB : (b + 1) * SB].reshape(SB // 8, 8, TILE)
                new = jnp.maximum(m, jnp.max(seen, axis=0))
                scale = jnp.exp(m - new)
                e = jnp.exp(seen - new[None])
                l = l * scale + jnp.sum(e, axis=0)
                d = d * scale + jnp.sum(e * grads, axis=0)
                m = new
                e_ref[rows, :] = e.reshape(SB, TILE)
                d_ref[rows, :] = grads.reshape(SB, TILE)
                m_ref[block] = m
            yield
        top = jnp.max(m, axis=0, keepdims=True)
        weight = jnp.exp(m - top)
        inv = 1.0 / jnp.sum(l * weight, axis=0, keepdims=True)
        yield jnp.broadcast_to(jnp.sum(d * weight, axis=0, keepdims=True) * inv, (8, TILE))
        for block in range(2 * CHIPS):
            m_ref[block] = jnp.exp(m_ref[block] - top) * inv

    def second_half(h, i, e_ref, d_ref, m_ref, dot):
        ts = pl.ds(pl.multiple_of(i * TILE, TILE), TILE)
        qzt, gzt = qz[h, ts, :], gz[h, ts, :]
        for c in range(CHIPS):
            probs, grads = [], []
            for b in range(2):
                block = 2 * c + b
                rows = slice(block * SB, (block + 1) * SB)
                prob = e_ref[rows, :].reshape(SB // 8, 8, TILE) * m_ref[block][None]
                grad = prob * (d_ref[rows, :].reshape(SB // 8, 8, TILE) - dot[None])
                probs.append(prob.reshape(SB, TILE).astype(BF16))
                grads.append(grad.reshape(SB, TILE).astype(BF16))
            cs = slice(c * CHUNK, (c + 1) * CHUNK)
            prob, grad = jnp.concatenate(probs, axis=0), jnp.concatenate(grads, axis=0)
            ds[h, cs, ts] = grad
            acc[cs, :] += jnp.dot(prob, gzt, preferred_element_type=F32) + jnp.dot(grad, qzt, preferred_element_type=F32)
            yield

    def last_chunk(c, e_ref, d_ref, m_ref, dot):
        ts = slice(TGT - TILE, TGT)
        probs, grads = [], []
        for b in range(2):
            block = 2 * c + b
            rows = pl.ds(pl.multiple_of(block * SB, SB), SB)
            prob = e_ref[rows, :].reshape(SB // 8, 8, TILE) * m_ref[block][None]
            grad = prob * (d_ref[rows, :].reshape(SB // 8, 8, TILE) - dot[None])
            probs.append(prob.reshape(SB, TILE).astype(BF16))
            grads.append(grad.reshape(SB, TILE).astype(BF16))
        cs = pl.ds(pl.multiple_of(c * CHUNK, CHUNK), CHUNK)
        prob, grad = jnp.concatenate(probs, axis=0), jnp.concatenate(grads, axis=0)
        ds[HEADS - 1, cs, ts] = grad
        value = jnp.dot(prob, gz[HEADS - 1, ts, :], preferred_element_type=F32)
        value = value + jnp.dot(grad, qz[HEADS - 1, ts, :], preferred_element_type=F32)
        return (acc[cs, :] + value).reshape(2, SB, 128)

    def chunk_out(r):
        c = chip_at(r, 1)
        return remote(part.at[HEADS - 1, c, 1 - core], sib.at[HEADS - 1, c], c_s.at[r], c_r.at[r], sibling)

    def pass_on(r):
        c = chip_at(r, 1)
        chunk_out(r).wait_recv()
        mid[HEADS - 1, c] = (own[c] + sib[HEADS - 1, c].astype(F32)).astype(BF16)
        if r:
            scatter_out(HEADS - 1, r).start()

    slot_a, slot_b = (e_a, d_a, m_a), (e_b, d_b, m_b)

    def step(ahead, behind):
        one = first_half(ahead[0], ahead[1], *ahead[2]) if ahead else None
        two = second_half(behind[0], behind[1], *behind[2], dots[behind[3]]) if behind else None
        for c in range(CHIPS):
            if one:
                next(one)
            if two:
                next(two)
        if one:
            dots[ahead[3]] = next(one)
            next(one, None)

    step((0, 0, slot_a, 0), None)

    def query_grad(h):
        kT[...] = kv[h].reshape(SRC, 128).T[:HD]
        dqT[h] = jnp.dot(kT[...], ds[h], preferred_element_type=F32) * HD**-0.5

    @pl.loop(0, HEADS * TILES // 2 - 1)
    def _(n):
        h, u = n // 2, lax.rem(n, 2)

        @pl.when(u == 0)
        def _():
            @pl.when(h < HEADS - 2)
            def _():
                for r in range(1, CHIPS):
                    gather_out(h + 2, r).start()

            @pl.when(h < HEADS - 1)
            def _():
                take_gathered(h + 1)

            acc[...] = jnp.zeros_like(acc)

        @pl.when(u == 1)
        def _():
            keys_ready(h + 1)

            @pl.when(h > 0)
            def _():
                mid_step(h - 1)

        step((h, 2 * u + 1, slot_b, 1), (h, 2 * u, slot_a, 0))
        after = 2 * n + 2
        step((after // TILES, lax.rem(after, TILES), slot_a, 0), (h, 2 * u + 1, slot_b, 1))

        @pl.when(u == 1)
        def _():
            both = acc[...].reshape(CHIPS, 2, SB, 128)
            part[h] = both.astype(BF16)
            own[...] = jnp.where(core == 0, both[:, 0], both[:, 1])
            to_sibling(h).start()

    mid_step(HEADS - 2)
    step((HEADS - 1, TILES - 1, slot_b, 1), (HEADS - 1, TILES - 2, slot_a, 0))
    last = HEADS - 1
    for n, r in enumerate(OWNERS):
        c = chip_at(r, 1)
        both = last_chunk(c, e_b, d_b, m_b, dots[1])
        part[last, c] = both.astype(BF16)
        own[c] = jnp.where(core == 0, both[0], both[1])
        chunk_out(r).start()
        if n >= LAG:
            pass_on(OWNERS[n - LAG])
    for r in OWNERS[CHIPS - LAG :]:
        pass_on(r)

    @pl.loop(0, 2)
    def _(h):
        query_grad(h)

    half = []
    for h in range(HEADS):
        total = mid[h, chip].astype(F32)
        for r in range(1, CHIPS):
            scatter_out(h, r).wait_recv()
            total = total + rs[h, r].astype(F32)
        half.append(total.T)

    half_k = jnp.concatenate([t[:HD] for t in half], axis=0).astype(BF16)
    half_v = jnp.concatenate([t[HD:] for t in half], axis=0).astype(BF16)
    loads[4].wait()
    loads[5].wait()

    def term(index):
        rows = pl.ds(pl.multiple_of(index * COLS, COLS), COLS)
        return jnp.dot(wk[rows, :], half_k, preferred_element_type=F32) + jnp.dot(wv[rows, :], half_v, preferred_element_type=F32)

    def send_across(r):
        xs[r] = term((1 - xh) * NZ + z_at(r)).astype(BF16)
        across(r).start()

    for r in (4, 3, 5):
        send_across(r)
    for r in (1, 7):
        zs[r] = term(xh * NZ + z_at(r)).astype(BF16)
        along(r).start()
        ys[r // 7] = term((1 - xh) * NZ + z_at(r)).astype(BF16)
        along_too(r).start()
    for r in (2, 6):
        send_across(r)
    query_grad(2)
    for r in (4, 3, 5):
        mine = term(xh * NZ + z_at(r))
        across(r).wait_recv()
        zs[r] = (mine + xr[r].astype(F32)).astype(BF16)
        relay(r).start()
    mine = term((1 - xh) * NZ + z)
    for r in (1, 7):
        along_too(r).wait_recv()
        mine = mine + yr[r // 7].astype(F32)
    xs[0] = mine.astype(BF16)
    across(0).start()
    query_grad(3)
    for r in (2, 6):
        mine = term(xh * NZ + z_at(r))
        across(r).wait_recv()
        mine = mine + xr[r].astype(F32)
        if r == 2:
            relay(3).wait_recv()
            relay(4).wait_recv()
            far = zl[1].astype(F32)
            mine = mine + zl[0].astype(F32) + jnp.where(core == 0, far, 0.0)
        else:
            relay(5).wait_recv()
            mine = mine + zl[2].astype(F32) + jnp.where(core == 1, far, 0.0)
        zs[r] = mine.astype(BF16)
        along(r).start()
    total = term(xh * NZ + z)
    dq[...] = dqT[...].reshape(FEAT, TGT).T.astype(BF16)
    across(0).wait_recv()
    total = total + xr[0].astype(F32)
    for r in NEAR:
        along(r).wait_recv()
        total = total + zr[r].astype(F32)
    mem[...] = total.T.astype(BF16)

    for h in range(HEADS):
        for r in range(1, CHIPS):
            gather_out(h, r).wait_send()
            scatter_out(h, r).wait_send()
        forward(h).wait_send()
    for h in range(HEADS - 1):
        to_sibling(h).wait_send()
    for r in range(CHIPS):
        chunk_out(r).wait_send()
    for r in (0, 2, 3, 4, 5, 6):
        across(r).wait_send()
    for r in NEAR:
        along(r).wait_send()
    for r in (3, 4, 5):
        relay(r).wait_send()
    for r in (1, 7):
        along_too(r).wait_send()


def attention(lag, toff, soff, q, g, k, v, wk, wv):
    vmem, smem, dma = pltpu.VMEM, pltpu.SMEM, pltpu.SemaphoreType.DMA
    return pl.pallas_call(
        kernel,
        out_shape=(jax.ShapeDtypeStruct((TGT, FEAT), BF16), jax.ShapeDtypeStruct((SB, COLS), BF16)),
        in_specs=[pl.BlockSpec(memory_space=smem)] * 3
        + [pl.BlockSpec(memory_space=pl.ANY)] * 6,
        out_specs=(pl.BlockSpec(memory_space=vmem),) * 2,
        scratch_shapes=[
            vmem((TGT, FEAT), BF16),
            vmem((TGT, FEAT), BF16),
            vmem((SB, FEAT), BF16),
            vmem((SB, FEAT), BF16),
            vmem((HEADS, 128, TGT), BF16),
            vmem((HEADS, 128, TGT), BF16),
            vmem((HEADS, TGT, 128), BF16),
            vmem((HEADS, TGT, 128), BF16),
            vmem((HEADS, CHIPS, 2, SB, 128), BF16),
            vmem((HD, SRC), BF16),
        ]
        + [vmem((SRC, TILE), F32), vmem((SRC, TILE), F32), vmem((2 * CHIPS, 8, TILE), F32)] * 2
        + [
            vmem((2, 8, TILE), F32),
            vmem((SRC, 128), F32),
            vmem((CHIPS, SB, 128), F32),
            vmem((HEADS, SRC, TGT), BF16),
            vmem((HEADS, HD, TGT), F32),
            vmem((HEADS, CHIPS, 2, SB, 128), BF16),
            vmem((HEADS, CHIPS, SB, 128), BF16),
            vmem((HEADS, CHIPS, SB, 128), BF16),
            vmem((HEADS, CHIPS, SB, 128), BF16),
            vmem((16 * COLS, FEAT), BF16),
            vmem((16 * COLS, FEAT), BF16),
        ]
        + [vmem((NZ, COLS, SB), BF16)] * 4
        + [vmem((3, COLS, SB), BF16)]
        + [vmem((2, COLS, SB), BF16)] * 2
        + [dma((HEADS, CHIPS))] * 2
        + [dma((HEADS,))] * 4
        + [dma((HEADS, CHIPS))] * 2
        + [dma((NZ,))] * 4
        + [dma((3,)), dma((6,))]
        + [dma((2,))] * 2
        + [dma((CHIPS,))] * 2,
        compiler_params=pltpu.CompilerParams(vmem_limit_bytes=58 * 2**20, collective_id=0, has_side_effects=True),
        name="wait_k_backward",
    )(lag, toff, soff, q, g, k, v, wk, wv)


def hand_over_kernel(dq_in, mem_in, dq, mem):
    dq[...] = dq_in[...]
    mem[...] = mem_in[...]


def hand_over(dq, mem):
    vmem = pl.BlockSpec(memory_space=pltpu.VMEM)
    return pl.pallas_call(
        hand_over_kernel,
        out_shape=(jax.ShapeDtypeStruct(dq.shape, dq.dtype), jax.ShapeDtypeStruct(mem.shape, mem.dtype)),
        in_specs=[vmem, vmem],
        out_specs=(vmem, vmem),
        name="hand_over",
    )(dq, mem)


def body(queries, key_states, value_states, grad_out, key_weight, value_weight, wait_lag, target_offset, source_offset):
    return hand_over(
        *attention(wait_lag, target_offset, source_offset, queries, grad_out, key_states, value_states, key_weight, value_weight)
    )


def solution(mesh):
    rows = P("seq", "head")
    in_specs = (rows, rows, rows, rows, P(None, "head"), P(None, "head"), P(), P(), P())
    return jax.shard_map(body, mesh=mesh, in_specs=in_specs, out_specs=(rows, rows), check_vma=False)
```

```python
import functools

import jax
import jax.numpy as jnp
from jax import lax
from jax.experimental import pallas as pl
from jax.experimental.pallas import tpu as pltpu
from jax.sharding import PartitionSpec as P

F32 = jnp.float32
BF16 = jnp.bfloat16
NEG = -1e30
HEADS, HD, TGT, SRC, SB, RATIO = 4, 64, 1024, 2048, 128, 8
FEAT = HEADS * HD
TILE = 256
TILES = TGT // TILE
CHUNK = 256
CHIPS = SRC // CHUNK
COLS = 256
NZ = 8
NEAR = (1, 7, 2, 6)
OWNERS = (5, 4, 3, 7, 2, 6, 1, 0)
LAG = 5
MESH = pl.DeviceIdType.MESH


def kernel(lag, toff, soff, q_hbm, g_hbm, k_hbm, v_hbm, wk_hbm, wv_hbm, dq, mem,
           q, g, k, v, qT, gT, qz, gz, kv, kT, e_a, d_a, m_a, e_b, d_b, m_b, dots, acc, own, ds, dqT, part, sib, mid, rs, wk, wv, xs, xr, zs, zr, zl, ys, yr,
           ag_s, ag_r, fw_s, fw_r, sb_s, sb_r, rs_s, rs_r, x_s, x_r, z_s, z_r, l_r, w_sem, y_s, y_r, c_s, c_r):
    me, head = lax.axis_index("seq"), lax.axis_index("head")
    y, xl, core = me // 4, lax.rem(me // 2, 2), lax.rem(me, 2)
    chip = me // 2
    xh, z = head // NZ, lax.rem(head, NZ)
    sibling = (chip * 2 + 1 - core, head)
    partner = (me, (1 - xh) * NZ + z)

    def chip_at(r, sign):
        return lax.rem(y + sign * (r // 2) + 4, 4) * 2 + (1 - xl if r % 2 else xl)

    def peer(r):
        return (chip_at(r, 1) * 2 + core, head)

    def z_at(r):
        return lax.rem(z + r, NZ)

    def z_peer(r):
        return (me, xh * NZ + z_at(r))

    loads = [
        pltpu.make_async_copy(src, dst, w_sem.at[n])
        for n, (src, dst) in enumerate(((k_hbm, k), (v_hbm, v), (q_hbm, q), (g_hbm, g), (wk_hbm, wk), (wv_hbm, wv)))
    ]
    barrier = pltpu.get_barrier_semaphore()
    for other in [sibling, partner] + [peer(r) for r in range(1, CHIPS)] + [z_peer(r) for r in NEAR]:
        pl.semaphore_signal(barrier, inc=1, device_id=other, device_id_type=MESH)
    for load in loads:
        load.start()

    def remote(src, dst, s_sem, r_sem, dev):
        return pltpu.make_async_remote_copy(src_ref=src, dst_ref=dst, send_sem=s_sem, recv_sem=r_sem, device_id=dev, device_id_type=MESH)

    def gather_out(h, r):
        return remote(kv.at[h, chip, core], kv.at[h, chip, core], ag_s.at[h, r], ag_r.at[h, r], peer(r))

    def gather_in(h, r):
        there = kv.at[h, chip_at(r, -1), core]
        return remote(there, there, ag_s.at[h, r], ag_r.at[h, r], peer(r))

    def forward(h):
        return remote(kv.at[h, :, core], kv.at[h, :, core], fw_s.at[h], fw_r.at[h], sibling)

    def forward_in(h):
        return remote(kv.at[h, :, 1 - core], kv.at[h, :, 1 - core], fw_s.at[h], fw_r.at[h], sibling)

    def to_sibling(h):
        return remote(part.at[h, :, 1 - core], sib.at[h], sb_s.at[h], sb_r.at[h], sibling)

    def scatter_out(h, r):
        return remote(mid.at[h, chip_at(r, 1)], rs.at[h, r], rs_s.at[h, r], rs_r.at[h, r], peer(r))

    def across(r):
        return remote(xs.at[r], xr.at[r], x_s.at[r], x_r.at[r], partner)

    def along(r):
        return remote(zs.at[r], zr.at[r], z_s.at[r], z_r.at[r], z_peer(r))

    def along_too(r):
        return remote(ys.at[r // 7], yr.at[r // 7], y_s.at[r // 7], y_r.at[r // 7], z_peer(r))

    def relay(r):
        step = 2 + 4 * core if r == 4 else 1 if r == 3 else 7
        return remote(zs.at[r], zl.at[r - 3], z_s.at[r], l_r.at[r - 3], z_peer(step))

    low = lax.broadcasted_iota(jnp.int32, (1, 128), 1) < HD

    def swapped(a):
        return jnp.concatenate([a[:, HD:], a[:, :HD]], axis=1)

    loads[0].wait()
    loads[1].wait()
    for p in range(HEADS // 2):
        kp, vp = k[:, p * 128 : (p + 1) * 128], v[:, p * 128 : (p + 1) * 128]
        kv[2 * p, chip, core] = jnp.where(low, kp, swapped(vp))
        kv[2 * p + 1, chip, core] = jnp.where(low, swapped(kp), vp)

    def prepare(p):
        qp = q[:, p * 128 : (p + 1) * 128] * jnp.asarray(HD**-0.5, BF16)
        gp = g[:, p * 128 : (p + 1) * 128]
        qt, gt = qp.T, gp.T
        none = jnp.zeros_like(qp)
        zero = jnp.zeros((HD, TGT), BF16)
        qs, gs = swapped(qp), swapped(gp)
        for j in range(2):
            h = p * 2 + j
            qz[h] = jnp.where(low, qs if j else qp, none)
            gz[h] = jnp.where(low, none, gp if j else gs)
            qT[h, :HD, :] = qt[j * HD : (j + 1) * HD]
            qT[h, HD:, :] = zero
            gT[h, :HD, :] = zero
            gT[h, HD:, :] = gt[j * HD : (j + 1) * HD]

    pl.semaphore_wait(barrier, 13)
    for r in range(1, CHIPS):
        gather_out(0, r).start()
    loads[2].wait()
    loads[3].wait()
    prepare(0)
    prepare(1)
    for r in range(1, CHIPS):
        gather_out(1, r).start()

    def take_gathered(h):
        for r in range(1, CHIPS):
            gather_in(h, r).wait_recv()
        forward(h).start()

    def keys_ready(h):
        forward_in(h).wait_recv()

    def mid_step(h):
        to_sibling(h).wait_recv()
        mid[h] = (own[...] + sib[h].astype(F32)).astype(BF16)
        for r in range(1, CHIPS):
            scatter_out(h, r).start()

    take_gathered(0)

    keys_ready(0)

    def first_half(h, i, e_ref, d_ref, m_ref):
        ts = pl.ds(pl.multiple_of(i * TILE, TILE), TILE)
        reach = RATIO * lag[0] + toff[me] + i * TILE + lax.broadcasted_iota(jnp.int32, (1, TILE), 1)
        step = RATIO * lax.broadcasted_iota(jnp.int32, (SB, TILE), 0)
        qt, gt = qT[h, :, ts], gT[h, :, ts]
        m = jnp.full((8, TILE), NEG, F32)
        l = jnp.zeros((8, TILE), F32)
        d = jnp.zeros((8, TILE), F32)
        for c in range(CHIPS):
            both = kv[h, c].reshape(CHUNK, 128)
            s = jnp.dot(both, qt, preferred_element_type=F32)
            dp = jnp.dot(both, gt, preferred_element_type=F32)
            for b in range(2):
                block = 2 * c + b
                rows = slice(block * SB, (block + 1) * SB)
                seen = jnp.where(step <= reach - RATIO * soff[block], s[b * SB : (b + 1) * SB], NEG).reshape(SB // 8, 8, TILE)
                grads = dp[b * SB : (b + 1) * SB].reshape(SB // 8, 8, TILE)
                new = jnp.maximum(m, jnp.max(seen, axis=0))
                scale = jnp.exp(m - new)
                e = jnp.exp(seen - new[None])
                l = l * scale + jnp.sum(e, axis=0)
                d = d * scale + jnp.sum(e * grads, axis=0)
                m = new
                e_ref[rows, :] = e.reshape(SB, TILE)
                d_ref[rows, :] = grads.reshape(SB, TILE)
                m_ref[block] = m
            yield
        top = jnp.max(m, axis=0, keepdims=True)
        weight = jnp.exp(m - top)
        inv = 1.0 / jnp.sum(l * weight, axis=0, keepdims=True)
        yield jnp.broadcast_to(jnp.sum(d * weight, axis=0, keepdims=True) * inv, (8, TILE))
        for block in range(2 * CHIPS):
            m_ref[block] = jnp.exp(m_ref[block] - top) * inv

    def second_half(h, i, e_ref, d_ref, m_ref, dot):
        ts = pl.ds(pl.multiple_of(i * TILE, TILE), TILE)
        qzt, gzt = qz[h, ts, :], gz[h, ts, :]
        for c in range(CHIPS):
            probs, grads = [], []
            for b in range(2):
                block = 2 * c + b
                rows = slice(block * SB, (block + 1) * SB)
                prob = e_ref[rows, :].reshape(SB // 8, 8, TILE) * m_ref[block][None]
                grad = prob * (d_ref[rows, :].reshape(SB // 8, 8, TILE) - dot[None])
                probs.append(prob.reshape(SB, TILE).astype(BF16))
                grads.append(grad.reshape(SB, TILE).astype(BF16))
            cs = slice(c * CHUNK, (c + 1) * CHUNK)
            prob, grad = jnp.concatenate(probs, axis=0), jnp.concatenate(grads, axis=0)
            ds[h, cs, ts] = grad
            acc[cs, :] += jnp.dot(prob, gzt, preferred_element_type=F32) + jnp.dot(grad, qzt, preferred_element_type=F32)
            yield

    def last_chunk(c, e_ref, d_ref, m_ref, dot):
        ts = slice(TGT - TILE, TGT)
        probs, grads = [], []
        for b in range(2):
            block = 2 * c + b
            rows = pl.ds(pl.multiple_of(block * SB, SB), SB)
            prob = e_ref[rows, :].reshape(SB // 8, 8, TILE) * m_ref[block][None]
            grad = prob * (d_ref[rows, :].reshape(SB // 8, 8, TILE) - dot[None])
            probs.append(prob.reshape(SB, TILE).astype(BF16))
            grads.append(grad.reshape(SB, TILE).astype(BF16))
        cs = pl.ds(pl.multiple_of(c * CHUNK, CHUNK), CHUNK)
        prob, grad = jnp.concatenate(probs, axis=0), jnp.concatenate(grads, axis=0)
        ds[HEADS - 1, cs, ts] = grad
        value = jnp.dot(prob, gz[HEADS - 1, ts, :], preferred_element_type=F32)
        value = value + jnp.dot(grad, qz[HEADS - 1, ts, :], preferred_element_type=F32)
        return (acc[cs, :] + value).reshape(2, SB, 128)

    def chunk_out(r):
        c = chip_at(r, 1)
        return remote(part.at[HEADS - 1, c, 1 - core], sib.at[HEADS - 1, c], c_s.at[r], c_r.at[r], sibling)

    def pass_on(r):
        c = chip_at(r, 1)
        chunk_out(r).wait_recv()
        mid[HEADS - 1, c] = (own[c] + sib[HEADS - 1, c].astype(F32)).astype(BF16)
        if r:
            scatter_out(HEADS - 1, r).start()

    slot_a, slot_b = (e_a, d_a, m_a), (e_b, d_b, m_b)

    def step(ahead, behind):
        one = first_half(ahead[0], ahead[1], *ahead[2]) if ahead else None
        two = second_half(behind[0], behind[1], *behind[2], dots[behind[3]]) if behind else None
        for c in range(CHIPS):
            if one:
                next(one)
            if two:
                next(two)
        if one:
            dots[ahead[3]] = next(one)
            next(one, None)

    step((0, 0, slot_a, 0), None)

    def query_grad(h):
        kT[...] = kv[h].reshape(SRC, 128).T[:HD]
        dqT[h] = jnp.dot(kT[...], ds[h], preferred_element_type=F32) * HD**-0.5

    @pl.loop(0, HEADS * TILES // 2 - 1)
    def _(n):
        h, u = n // 2, lax.rem(n, 2)

        @pl.when(u == 0)
        def _():
            @pl.when(h < HEADS - 2)
            def _():
                for r in range(1, CHIPS):
                    gather_out(h + 2, r).start()

            @pl.when(h < HEADS - 1)
            def _():
                take_gathered(h + 1)

            acc[...] = jnp.zeros_like(acc)

        @pl.when(u == 1)
        def _():
            keys_ready(h + 1)

            @pl.when(h > 0)
            def _():
                mid_step(h - 1)

        step((h, 2 * u + 1, slot_b, 1), (h, 2 * u, slot_a, 0))
        after = 2 * n + 2
        step((after // TILES, lax.rem(after, TILES), slot_a, 0), (h, 2 * u + 1, slot_b, 1))

        @pl.when(u == 1)
        def _():
            both = acc[...].reshape(CHIPS, 2, SB, 128)
            part[h] = both.astype(BF16)
            own[...] = jnp.where(core == 0, both[:, 0], both[:, 1])
            to_sibling(h).start()

    mid_step(HEADS - 2)
    step((HEADS - 1, TILES - 1, slot_b, 1), (HEADS - 1, TILES - 2, slot_a, 0))
    last = HEADS - 1
    for n, r in enumerate(OWNERS):
        c = chip_at(r, 1)
        both = last_chunk(c, e_b, d_b, m_b, dots[1])
        part[last, c] = both.astype(BF16)
        own[c] = jnp.where(core == 0, both[0], both[1])
        chunk_out(r).start()
        if n >= LAG:
            pass_on(OWNERS[n - LAG])
    for r in OWNERS[CHIPS - LAG :]:
        pass_on(r)

    @pl.loop(0, HEADS)
    def _(h):
        query_grad(h)

    half = []
    for h in range(HEADS):
        total = mid[h, chip].astype(F32)
        for r in range(1, CHIPS):
            scatter_out(h, r).wait_recv()
            total = total + rs[h, r].astype(F32)
        half.append(total.T)

    half_k = jnp.concatenate([t[:HD] for t in half], axis=0).astype(BF16)
    half_v = jnp.concatenate([t[HD:] for t in half], axis=0).astype(BF16)
    loads[4].wait()
    loads[5].wait()

    def term(index):
        rows = pl.ds(pl.multiple_of(index * COLS, COLS), COLS)
        return jnp.dot(wk[rows, :], half_k, preferred_element_type=F32) + jnp.dot(wv[rows, :], half_v, preferred_element_type=F32)

    def send_across(r):
        xs[r] = term((1 - xh) * NZ + z_at(r)).astype(BF16)
        across(r).start()

    for r in (4, 3, 5):
        send_across(r)
    for r in (1, 7):
        zs[r] = term(xh * NZ + z_at(r)).astype(BF16)
        along(r).start()
        ys[r // 7] = term((1 - xh) * NZ + z_at(r)).astype(BF16)
        along_too(r).start()
    for r in (2, 6):
        send_across(r)
    for r in (4, 3, 5):
        mine = term(xh * NZ + z_at(r))
        across(r).wait_recv()
        zs[r] = (mine + xr[r].astype(F32)).astype(BF16)
        relay(r).start()
    mine = term((1 - xh) * NZ + z)
    for r in (1, 7):
        along_too(r).wait_recv()
        mine = mine + yr[r // 7].astype(F32)
    xs[0] = mine.astype(BF16)
    across(0).start()
    for r in (2, 6):
        mine = term(xh * NZ + z_at(r))
        across(r).wait_recv()
        mine = mine + xr[r].astype(F32)
        if r == 2:
            relay(3).wait_recv()
            relay(4).wait_recv()
            far = zl[1].astype(F32)
            mine = mine + zl[0].astype(F32) + jnp.where(core == 0, far, 0.0)
        else:
            relay(5).wait_recv()
            mine = mine + zl[2].astype(F32) + jnp.where(core == 1, far, 0.0)
        zs[r] = mine.astype(BF16)
        along(r).start()
    total = term(xh * NZ + z)
    dq[...] = dqT[...].reshape(FEAT, TGT).T.astype(BF16)
    across(0).wait_recv()
    total = total + xr[0].astype(F32)
    for r in NEAR:
        along(r).wait_recv()
        total = total + zr[r].astype(F32)
    mem[...] = total.T.astype(BF16)

    for h in range(HEADS):
        for r in range(1, CHIPS):
            gather_out(h, r).wait_send()
            scatter_out(h, r).wait_send()
        forward(h).wait_send()
    for h in range(HEADS - 1):
        to_sibling(h).wait_send()
    for r in range(CHIPS):
        chunk_out(r).wait_send()
    for r in (0, 2, 3, 4, 5, 6):
        across(r).wait_send()
    for r in NEAR:
        along(r).wait_send()
    for r in (3, 4, 5):
        relay(r).wait_send()
    for r in (1, 7):
        along_too(r).wait_send()


def attention(lag, toff, soff, q, g, k, v, wk, wv):
    vmem, smem, dma = pltpu.VMEM, pltpu.SMEM, pltpu.SemaphoreType.DMA
    return pl.pallas_call(
        kernel,
        out_shape=(jax.ShapeDtypeStruct((TGT, FEAT), BF16), jax.ShapeDtypeStruct((SB, COLS), BF16)),
        in_specs=[pl.BlockSpec(memory_space=smem)] * 3
        + [pl.BlockSpec(memory_space=pl.ANY)] * 6,
        out_specs=(pl.BlockSpec(memory_space=vmem),) * 2,
        scratch_shapes=[
            vmem((TGT, FEAT), BF16),
            vmem((TGT, FEAT), BF16),
            vmem((SB, FEAT), BF16),
            vmem((SB, FEAT), BF16),
            vmem((HEADS, 128, TGT), BF16),
            vmem((HEADS, 128, TGT), BF16),
            vmem((HEADS, TGT, 128), BF16),
            vmem((HEADS, TGT, 128), BF16),
            vmem((HEADS, CHIPS, 2, SB, 128), BF16),
            vmem((HD, SRC), BF16),
        ]
        + [vmem((SRC, TILE), F32), vmem((SRC, TILE), F32), vmem((2 * CHIPS, 8, TILE), F32)] * 2
        + [
            vmem((2, 8, TILE), F32),
            vmem((SRC, 128), F32),
            vmem((CHIPS, SB, 128), F32),
            vmem((HEADS, SRC, TGT), BF16),
            vmem((HEADS, HD, TGT), F32),
            vmem((HEADS, CHIPS, 2, SB, 128), BF16),
            vmem((HEADS, CHIPS, SB, 128), BF16),
            vmem((HEADS, CHIPS, SB, 128), BF16),
            vmem((HEADS, CHIPS, SB, 128), BF16),
            vmem((16 * COLS, FEAT), BF16),
            vmem((16 * COLS, FEAT), BF16),
        ]
        + [vmem((NZ, COLS, SB), BF16)] * 4
        + [vmem((3, COLS, SB), BF16)]
        + [vmem((2, COLS, SB), BF16)] * 2
        + [dma((HEADS, CHIPS))] * 2
        + [dma((HEADS,))] * 4
        + [dma((HEADS, CHIPS))] * 2
        + [dma((NZ,))] * 4
        + [dma((3,)), dma((6,))]
        + [dma((2,))] * 2
        + [dma((CHIPS,))] * 2,
        compiler_params=pltpu.CompilerParams(vmem_limit_bytes=58 * 2**20, collective_id=0, has_side_effects=True),
        name="wait_k_backward",
    )(lag, toff, soff, q, g, k, v, wk, wv)


def hand_over_kernel(dq_in, mem_in, dq, mem):
    dq[...] = dq_in[...]
    mem[...] = mem_in[...]


def hand_over(dq, mem):
    vmem = pl.BlockSpec(memory_space=pltpu.VMEM)
    return pl.pallas_call(
        hand_over_kernel,
        out_shape=(jax.ShapeDtypeStruct(dq.shape, dq.dtype), jax.ShapeDtypeStruct(mem.shape, mem.dtype)),
        in_specs=[vmem, vmem],
        out_specs=(vmem, vmem),
        name="hand_over",
    )(dq, mem)


def body(queries, key_states, value_states, grad_out, key_weight, value_weight, wait_lag, target_offset, source_offset):
    return hand_over(
        *attention(wait_lag, target_offset, source_offset, queries, grad_out, key_states, value_states, key_weight, value_weight)
    )


def solution(mesh):
    rows = P("seq", "head")
    in_specs = (rows, rows, rows, rows, P(None, "head"), P(None, "head"), P(), P(), P())
    return jax.shard_map(body, mesh=mesh, in_specs=in_specs, out_specs=(rows, rows), check_vma=False)
```
